128 devices in a mesh: grp: 2 (over y_hi), seq: 64 (over x, z, y_lo, core).
Axes of the slice: x: 4, y: 4 (y_hi: 2, y_lo: 2; y = y_hi * 2 + y_lo), z: 4, core: 2. Of those that a mesh axis runs over, the one named last changes fastest.
Arguments:
- queries: bfloat16 [16384, 2048], P(('grp', 'seq')), parts along dimension 0, may hold values from -150 to 150
- keys: bfloat16 [16384, 1024], P(('grp', 'seq')), parts along dimension 0, may hold values from -6 to 6
- values: bfloat16 [16384, 1024], P(('grp', 'seq')), parts along dimension 0, may hold values from -6 to 6
- dout: bfloat16 [16384, 2048], P(('grp', 'seq')), parts along dimension 0, may hold values from -6 to 6
- tail_keys: bfloat16 [2048, 1024], P(('grp', 'seq')), parts along dimension 0, may hold values from -6 to 6
- tail_values: bfloat16 [2048, 1024], P(('grp', 'seq')), parts along dimension 0, may hold values from -6 to 6
- lengths: int32 [4], P('grp'), parts along dimension 0, may hold values from 1 to 6144, 8192 in all
Outputs:
- grad_queries: bfloat16 [16384, 2048], P(('grp', 'seq')), parts along dimension 0
- grad_keys: bfloat16 [16384, 1024], P(('grp', 'seq')), parts along dimension 0
- grad_values: bfloat16 [16384, 1024], P(('grp', 'seq')), parts along dimension 0
- grad_tail_keys: bfloat16 [2048, 1024], P(('grp', 'seq')), parts along dimension 0
- grad_tail_values: bfloat16 [2048, 1024], P(('grp', 'seq')), parts along dimension 0
The draws below stay inside these ranges and needn't reach their ends.
There are 2 independent parts, one for each index of `grp`. The reference program is written for one: setup_inputs(seed, part) draws one part's arguments, and reference() takes and returns one part's arrays. A program takes and returns all parts, laid end to end along the dimension named above; each array names one. Nothing has to cross between parts.
All inputs are finite; a program needn't handle non-finite values.
Results may differ from the reference program's by a relative error of at most 0.039.
Values may be sent and summed in bfloat16 or wider, within the bound.
A program may use at most 128 MiB of HBM per device.

```python
import math
import jax
import jax.numpy as jnp
import numpy as np
from jax import lax

H = 16
KVH = 8
HD = 128
W = 1024
ROLLOUTS = 2
TOK_DEV = 128
TOKENS = 8192


def shared_keys(key):
    return jnp.clip(jax.random.normal(key, (TOKENS, KVH * HD), jnp.float32), -6.0, 6.0)


def draw_keys(key, part):
    return shared_keys(key).astype(jnp.bfloat16)


def draw_queries(key, part):
    key = jax.random.fold_in(key, 11)
    fresh = jnp.clip(jax.random.normal(key, (TOKENS, H * HD), jnp.float32), -6.0, 6.0)
    return fresh.astype(jnp.bfloat16)


def block_scale(key, extent, pieces, smallest, largest):
    def one(axis_at, shards_of):
        steps = jax.random.uniform(jax.random.fold_in(jax.random.fold_in(key, 6), axis_at), (shards_of,), jnp.float32, smallest / len(pieces), largest / len(pieces))
        return jnp.repeat(jnp.exp(steps), extent[axis_at] // shards_of).reshape((-1,) + (1,) * (len(extent) - axis_at - 1))

    factor_of = one(*pieces[0])
    for cut in pieces[1:]:
        factor_of = factor_of * one(*cut)
    return factor_of


def profile(amount, total, bound, slope):
    loads = [(1 << 20) // math.isqrt(grade ** slope) + 1 for grade in range(2, amount + 1)]
    spare, given = total - bound - (amount - 1), [1] * (amount - 1)
    while spare > 0:
        candidates = [i for i in range(amount - 1) if given[i] < bound]
        pool, left = sum([loads[i] for i in candidates]), spare
        for i in candidates:
            addition = min(bound - given[i], max(1, left * loads[i] // pool), spare)
            given[i] = given[i] + addition
            spare = spare - addition
    return np.array([bound] + given)


def ragged_sizes(stream_key, amount, total, reach, skew):
    if amount == 2:
        one = jax.random.randint(stream_key, (), max(1, total - reach), min(reach, total - 1) + 1)
        return jnp.stack([one, total - one])
    sizes = jnp.asarray(profile(amount, total, reach, skew), jnp.int32)
    couples = (amount - 1) // 2
    source_of, receiver = sizes[1:1 + 2 * couples:2], sizes[2:2 + 2 * couples:2]
    margin = jnp.minimum(source_of - 1, reach - receiver)
    passed = jax.random.randint(jax.random.fold_in(stream_key, 1), (couples,), 0, 1 << 20) % (margin + 1)
    sizes = sizes.at[1:1 + 2 * couples:2].set(source_of - passed).at[2:2 + 2 * couples:2].set(receiver + passed)
    return sizes[jax.random.permutation(jax.random.fold_in(stream_key, 2), amount)]


def scatter_about(stream_key, dims, spread, reach, shards=(), dtype=jnp.bfloat16):
    factor_of = block_scale(stream_key, dims, shards, -0.22, 0.18) if shards else 1.0
    entries = jax.random.normal(stream_key, dims, jnp.float32) * spread * factor_of
    return jnp.minimum(jnp.maximum(entries, -reach), reach).astype(dtype)


def setup_inputs(seed: int = 0, part: int = 0) -> dict:
    splits = jax.random.split(jax.random.key(seed), 8)
    part_keys = jax.random.split(jax.random.fold_in(splits[7], part), 8)
    return {
        "queries": draw_queries(jax.random.fold_in(jax.random.fold_in(splits[7], part), 71), part),
        "keys": draw_keys(jax.random.fold_in(jax.random.fold_in(splits[7], part), 71), part),
        "values": scatter_about(part_keys[2], (TOKENS, KVH * HD), 1.0, 6.0, ((0, 64),)),
        "dout": scatter_about(part_keys[3], (TOKENS, H * HD), 1.0, 6.0, ((0, 64),)),
        "tail_keys": scatter_about(part_keys[4], (W, KVH * HD), 1.0, 6.0, ((0, 64),)),
        "tail_values": scatter_about(part_keys[5], (W, KVH * HD), 1.0, 6.0, ((0, 64),)),
        "lengths": ragged_sizes(part_keys[6], ROLLOUTS, TOKENS, 3 * TOKENS // (2 * ROLLOUTS), 2).astype(jnp.int32),
    }


qscale = 168.0 ** -0.5
neg_big = -1.0e30


def token_place(glob_rows, lengths):
    finish = jnp.cumsum(lengths).astype(jnp.int32)
    starts = (finish - lengths).astype(jnp.int32)
    rollout = jnp.sum((finish[None, :] <= glob_rows[:, None]).astype(jnp.int32), axis=1).astype(jnp.int32)
    indices = jnp.arange(lengths.shape[0]).astype(jnp.int32)
    anchor = jnp.sum(jnp.where(indices[None, :] == rollout[:, None], starts[None, :], 0), axis=1).astype(jnp.int32)
    rollout = jnp.where(glob_rows < 0, -1, rollout).astype(jnp.int32)
    return rollout, (glob_rows - anchor).astype(jnp.int32)


def window_mask(query_glob, query_roll, key_glob, key_roll):
    distance = query_glob[:, None] - key_glob[None, :]
    return (query_roll[:, None] == key_roll[None, :]) & (distance >= 0) & (distance < W)


def tail_mask(query_pos):
    return jnp.arange(W).astype(jnp.int32)[None, :] > query_pos[:, None]


def full_block(query_heads, dout_heads, key_rows, value_rows, visible):
    queried = query_heads.astype(jnp.float32)
    douts = dout_heads.astype(jnp.float32)
    keyset = key_rows.reshape(key_rows.shape[0], KVH, HD).astype(jnp.float32)
    valset = value_rows.reshape(value_rows.shape[0], KVH, HD).astype(jnp.float32)
    live = visible[None, None]
    logits = jnp.einsum("rkgd,ckd->kgrc", queried, keyset) * qscale
    run_max = jnp.max(jnp.where(live, logits, neg_big), axis=3, keepdims=True)
    run_sum = jnp.sum(jnp.where(live, jnp.exp(logits - run_max), 0.0), axis=3, keepdims=True)
    log_total = run_max + jnp.log(run_sum)
    attend = jnp.where(live, jnp.exp(logits - log_total), 0.0)
    dweight = jnp.einsum("rkgd,ckd->kgrc", douts, valset)
    deltas = jnp.sum(attend * dweight, axis=3, keepdims=True)
    dscores = lax.optimization_barrier((attend * (dweight - deltas)).astype(jnp.bfloat16)).astype(jnp.float32)
    rounded = lax.optimization_barrier(attend.astype(jnp.bfloat16)).astype(jnp.float32)
    query_grad = jnp.einsum("kgrc,ckd->rkgd", dscores, keyset) * qscale
    key_grad = jnp.einsum("kgrc,rkgd->ckd", dscores, queried) * qscale
    value_grad = jnp.einsum("kgrc,rkgd->ckd", rounded, douts)
    return query_grad, key_grad.reshape(key_rows.shape[0], KVH * HD), value_grad.reshape(key_rows.shape[0], KVH * HD)


def reference(queries, keys, values, dout, tail_keys, tail_values, lengths):
    row_count = TOK_DEV
    groups = H // KVH
    block_count = queries.shape[0] // row_count
    keys_pad = jnp.concatenate([jnp.zeros((W, KVH * HD), jnp.bfloat16), keys], axis=0)
    values_pad = jnp.concatenate([jnp.zeros((W, KVH * HD), jnp.bfloat16), values], axis=0)

    def step(carried, block_index):
        key_accum, value_accum, tail_key_accum, tail_value_accum = carried
        first_row = (block_index * row_count).astype(jnp.int32)
        query_glob = (first_row + jnp.arange(row_count).astype(jnp.int32)).astype(jnp.int32)
        query_roll, query_pos = token_place(query_glob, lengths)
        key_glob = (first_row - W + jnp.arange(W + row_count).astype(jnp.int32)).astype(jnp.int32)
        key_roll, key_pos = token_place(key_glob, lengths)
        window_keys = lax.dynamic_slice_in_dim(keys_pad, first_row, W + row_count, 0)
        window_values = lax.dynamic_slice_in_dim(values_pad, first_row, W + row_count, 0)
        query_heads = lax.dynamic_slice_in_dim(queries, first_row, row_count, 0).reshape(row_count, KVH, groups, HD)
        dout_heads = lax.dynamic_slice_in_dim(dout, first_row, row_count, 0).reshape(row_count, KVH, groups, HD)
        visible = jnp.concatenate([tail_mask(query_pos), window_mask(query_glob, query_roll, key_glob, key_roll)], axis=1)
        all_keys = jnp.concatenate([tail_keys, window_keys], axis=0)
        all_values = jnp.concatenate([tail_values, window_values], axis=0)
        query_grad, key_grad, value_grad = full_block(query_heads, dout_heads, all_keys, all_values, visible)
        old_keys = lax.dynamic_slice_in_dim(key_accum, first_row, W + row_count, 0)
        old_values = lax.dynamic_slice_in_dim(value_accum, first_row, W + row_count, 0)
        key_accum = lax.dynamic_update_slice_in_dim(key_accum, old_keys + key_grad[W:], first_row, 0)
        value_accum = lax.dynamic_update_slice_in_dim(value_accum, old_values + value_grad[W:], first_row, 0)
        tail_key_accum = tail_key_accum + key_grad[:W]
        tail_value_accum = tail_value_accum + value_grad[:W]
        return (key_accum, value_accum, tail_key_accum, tail_value_accum), query_grad.astype(jnp.bfloat16)

    initial = (jnp.zeros((W + queries.shape[0], KVH * HD), jnp.float32), jnp.zeros((W + queries.shape[0], KVH * HD), jnp.float32), jnp.zeros((W, KVH * HD), jnp.float32), jnp.zeros((W, KVH * HD), jnp.float32))
    finals, query_blocks = lax.scan(step, initial, jnp.arange(block_count).astype(jnp.int32))
    key_accum, value_accum, tail_key_accum, tail_value_accum = finals
    grad_queries = query_blocks.reshape(queries.shape[0], H * HD)
    return (grad_queries, key_accum[W:].astype(jnp.bfloat16), value_accum[W:].astype(jnp.bfloat16), tail_key_accum.astype(jnp.bfloat16), tail_value_accum.astype(jnp.bfloat16))
```

```python
import math

import jax
import jax.numpy as jnp
from jax import lax
from jax.experimental import pallas as pl
from jax.experimental.pallas import tpu as pltpu
from jax.sharding import PartitionSpec as P


KVH = 8
HD = 128
W = 1024
ROWS = 128
COHORT = 8
PAIR = 2 * HD
BAND = W + ROWS
STREAM = 2 * W
CHUNKS = BAND // ROWS
SCALE = 168.0 ** -0.5
SCALE2 = SCALE * math.log2(math.e)
NEG = -1.0e30
F32 = jnp.float32
BF16 = jnp.bfloat16
MESH = pl.DeviceIdType.MESH


def dot_nt(a, b):
    return lax.dot_general(a, b, (((1,), (1,)), ((), ())), preferred_element_type=F32)


def dot_nn(a, b):
    return jnp.dot(a, b, preferred_element_type=F32)


def at128(index, count=ROWS):
    return pl.ds(index * ROWS, count)


def kernel(len_ref, q_ref, do_ref, k_ref, v_ref, tk_ref, tv_ref,
           dq_ref, dk_ref, dv_ref, dtk_ref, dtv_ref,
           qb, dob, kv, tkv, kt, sc, dpc, ds, pr, acc, side, dqx,
           back, hsend, hrecv, osend, dqs, tsend, trecv, tfin,
           in_send, in_recv, halo_sem, tg_send, tg_recv,
           hg_send, hg_recv, tr_send, tr_recv, out_send, out_recv):
    me = lax.axis_index("seq")
    g = me // COHORT
    e = me % COHORT
    flip = 4 * (g % 2)
    h = (e + flip) % COHORT
    t0 = g * W

    def peer(t):
        return g * COHORT + (e + t) % COHORT

    def same_head(gg):
        return gg * COHORT + (h + 4 * (gg % 2)) % COHORT

    barrier = pltpu.get_barrier_semaphore()

    def greet(t, carry):
        pl.semaphore_signal(barrier, inc=1, device_id={"seq": peer(t)}, device_id_type=MESH)
        pl.semaphore_signal(barrier, inc=1, device_id={"seq": same_head((g + t) % COHORT)}, device_id_type=MESH)
        return carry

    lax.fori_loop(1, COHORT, greet, 0)
    pl.semaphore_wait(barrier, 2 * (COHORT - 1))

    left, right = pl.ds(0, HD), pl.ds(HD, HD)

    def placed(kind, head, source):
        tail_rows = pl.ds(pl.multiple_of(g * ROWS + source * 16, 16), 16)
        own = at128(COHORT + source)
        return (
            (k_ref.at[:, at128(head)], kv.at[own, left]),
            (v_ref.at[:, at128(head)], kv.at[own, right]),
            (tk_ref.at[:, at128(head)], tkv.at[tail_rows, left]),
            (tv_ref.at[:, at128(head)], tkv.at[tail_rows, right]),
            (q_ref.at[:, at128(2 * head, PAIR)], qb.at[at128(source), :]),
            (do_ref.at[:, at128(2 * head, PAIR)], dob.at[at128(source), :]),
        )[kind]

    def give(kind, t):
        to = (e + t) % COHORT
        src, dst = placed(kind, (to + flip) % COHORT, e)
        return pltpu.make_async_remote_copy(
            src_ref=src, dst_ref=dst, send_sem=in_send.at[kind, t], recv_sem=in_recv.at[kind, e],
            device_id={"seq": peer(t)}, device_id_type=MESH)

    def take(kind, t):
        source = (e + t) % COHORT
        src, dst = placed(kind, h, source)
        return pltpu.make_async_remote_copy(
            src_ref=src, dst_ref=dst, send_sem=in_send.at[kind, t], recv_sem=in_recv.at[kind, source],
            device_id={"seq": peer(t)}, device_id_type=MESH)

    def keep(kind):
        src, dst = placed(kind, h, e)
        return pltpu.make_async_copy(src, dst, in_recv.at[kind, e])

    def give_all(kinds):
        def body(t, carry):
            for kind in kinds:
                give(kind, t).start()
            return carry
        lax.fori_loop(1, COHORT, body, 0)
        for kind in kinds:
            keep(kind).start()

    def take_all(kinds):
        def body(t, carry):
            for kind in kinds:
                take(kind, t).wait_recv()
            return carry
        for kind in kinds:
            keep(kind).wait()
        lax.fori_loop(1, COHORT, body, 0)

    give_all((0, 1))
    give_all((2, 3))
    give_all((4, 5))

    take_all((0, 1))
    halo = pltpu.make_async_remote_copy(
        src_ref=kv.at[pl.ds(W, W), :], dst_ref=kv.at[pl.ds(0, W), :],
        send_sem=halo_sem.at[0], recv_sem=halo_sem.at[1],
        device_id={"seq": same_head((g + 1) % COHORT)}, device_id_type=MESH)
    halo.start()

    take_all((2, 3))

    def tail_give(t):
        return pltpu.make_async_remote_copy(
            src_ref=tkv.at[at128(g), :], dst_ref=tkv.at[at128(g), :],
            send_sem=tg_send.at[t], recv_sem=tg_recv.at[g],
            device_id={"seq": same_head((g + t) % COHORT)}, device_id_type=MESH)

    def tail_take(t):
        gg = (g + t) % COHORT
        return pltpu.make_async_remote_copy(
            src_ref=tkv.at[at128(gg), :], dst_ref=tkv.at[at128(gg), :],
            send_sem=tg_send.at[t], recv_sem=tg_recv.at[gg],
            device_id={"seq": same_head(gg)}, device_id_type=MESH)

    def start_tail(t, carry):
        tail_give(t).start()
        return carry

    def wait_tail(t, carry):
        tail_take(t).wait_recv()
        return carry

    lax.fori_loop(1, COHORT, start_tail, 0)
    lax.fori_loop(1, COHORT, wait_tail, 0)
    halo.wait_recv()

    @pl.when(g == 0)
    def _():
        kv[0:W, :] = tkv[...]

    first = len_ref[0]
    delta = first - t0
    whole = lax.shift_right_arithmetic(delta, 7)
    part = delta - whole * ROWS
    shift_row = lax.broadcasted_iota(jnp.int32, (ROWS, 2 * ROWS), 0)
    shift_col = lax.broadcasted_iota(jnp.int32, (ROWS, 2 * ROWS), 1)
    forth = (shift_col == shift_row + (ROWS - part)).astype(F32).astype(BF16)
    stream_row = lax.broadcasted_iota(jnp.int32, (ROWS, PAIR), 0)

    def second_stream(n, carry):
        low = jnp.clip(n - whole - 1, 0, COHORT - 1)
        high = jnp.clip(n - whole, 0, COHORT - 1)
        moved = (dot_nn(forth[:, :ROWS], tkv[at128(low), :])
                 + dot_nn(forth[:, ROWS:], tkv[at128(high), :]))
        plain = kv[at128(n), :]
        mixed = jnp.where(n * ROWS + stream_row < delta + W, moved, plain.astype(F32)).astype(BF16)
        kv[at128(16 + n), :] = mixed
        kt[:, at128(n)] = plain[:, :HD].T
        kt[:, at128(16 + n)] = mixed[:, :HD].T
        return carry

    lax.fori_loop(0, 16, second_stream, 0)

    take_all((4, 5))

    key_row = lax.broadcasted_iota(jnp.int32, (ROWS, PAIR), 0)
    query_row = lax.broadcasted_iota(jnp.int32, (ROWS, PAIR), 1) % ROWS
    lane_row = lax.broadcasted_iota(jnp.int32, (1, PAIR), 1) % ROWS

    def stacked(ref, block):
        rows = at128(block)
        return jnp.concatenate([ref[rows, :HD], ref[rows, HD:]], axis=0)

    def attend(block, start, valid):
        queries, douts = stacked(qb, block), stacked(dob, block)
        top = None
        for c in range(CHUNKS):
            logits = dot_nt(kv[at128(start + c), :HD], queries)
            if c == 0:
                logits = jnp.where(key_row > query_row, logits, NEG)
            if c == CHUNKS - 1:
                logits = jnp.where(key_row <= query_row, logits, NEG)
            sc[c * ROWS:(c + 1) * ROWS, :] = logits
            most = jnp.max(logits, axis=0, keepdims=True)
            top = most if top is None else jnp.maximum(top, most)
        total = jnp.zeros((1, PAIR), F32)
        mixed = jnp.zeros((1, PAIR), F32)
        for c in range(CHUNKS):
            rows = slice(c * ROWS, (c + 1) * ROWS)
            weight = jnp.exp2((sc[rows, :] - top) * SCALE2)
            dprob = dot_nt(kv[at128(start + c), HD:], douts)
            sc[rows, :] = weight
            dpc[rows, :] = dprob
            total = total + jnp.sum(weight, axis=0, keepdims=True)
            mixed = mixed + jnp.sum(weight * dprob, axis=0, keepdims=True)
        inverse = valid / total
        deltas = mixed / total
        for c in range(CHUNKS):
            rows = slice(c * ROWS, (c + 1) * ROWS)
            probs = sc[rows, :] * inverse
            pr[rows, :] = probs.astype(BF16)
            ds[rows, :] = (probs * (dpc[rows, :] - deltas)).astype(BF16)
        dq_t = dot_nn(kt[:, at128(start, BAND)], ds[...]) * SCALE
        return queries, douts, jnp.concatenate([dq_t[:, :HD].T, dq_t[:, HD:].T], axis=1)

    cut = jnp.clip(whole, 0, COHORT - 1)
    cut_row = lane_row + cut * ROWS
    in_cut = ((cut_row >= delta) & (cut * ROWS < delta)).astype(F32)
    queries, douts, dqx[...] = attend(cut, 16 + cut, in_cut)
    for c in range(CHUNKS):
        rows = slice(c * ROWS, (c + 1) * ROWS)
        side[rows, :HD] = dot_nn(ds[rows, :], queries)
        side[rows, HD:] = dot_nn(pr[rows, :], douts)

    def clear(n, carry):
        away = n - cut
        inside = ((away >= 0) & (away < CHUNKS)).astype(F32)
        acc[0, at128(n), :] = jnp.zeros((ROWS, PAIR), F32)
        acc[1, at128(n), :] = side[at128(jnp.clip(away, 0, CHUNKS - 1)), :] * inside
        return carry

    lax.fori_loop(0, 16, clear, 0)

    half = lax.broadcasted_iota(jnp.int32, (1, PAIR), 1)
    by_half = jnp.where(half < HD, SCALE, 1.0).astype(F32)

    def token_part(n):
        later = n * ROWS + stream_row >= delta + W
        return (acc[0, at128(n), :] + jnp.where(later, acc[1, at128(n), :], 0.0)) * by_half

    def send_dq(i):
        return pltpu.make_async_remote_copy(
            src_ref=dqs.at[at128(i), :], dst_ref=dq_ref.at[:, at128(2 * h, PAIR)],
            send_sem=out_send.at[0, i], recv_sem=out_recv.at[0, e],
            device_id={"seq": g * COHORT + i}, device_id_type=MESH)

    def send_halo_grad(i):
        return pltpu.make_async_remote_copy(
            src_ref=hsend.at[at128(i), :], dst_ref=hrecv.at[at128(i), :],
            send_sem=hg_send.at[i], recv_sem=hg_recv.at[i],
            device_id={"seq": same_head((g + COHORT - 1) % COHORT)}, device_id_type=MESH)

    has_halo = (g > 0).astype(F32)

    def main(i, carry):
        second = (i * ROWS >= delta).astype(jnp.int32)
        second_f = second.astype(F32)
        valid = jnp.maximum((lane_row + i * ROWS < delta).astype(F32), second_f)
        queries, douts, dq = attend(i, 16 * second + i, valid)
        for c in range(CHUNKS):
            rows = slice(c * ROWS, (c + 1) * ROWS)
            dkc = dot_nn(ds[rows, :], queries)
            dvc = dot_nn(pr[rows, :], douts)
            to = at128(i + c)
            acc[0, to, :HD] += dkc * (1.0 - second_f)
            acc[0, to, HD:] += dvc * (1.0 - second_f)
            acc[1, to, :HD] += dkc * second_f
            acc[1, to, HD:] += dvc * second_f
        dqs[at128(i), :] = (dq + dqx[...] * (cut == i).astype(F32)).astype(BF16)

        @pl.when(i != e)
        def _():
            send_dq(i).start()

        hsend[at128(i), :] = (token_part(i) * has_halo).astype(BF16)
        send_halo_grad(i).start()
        return carry

    lax.fori_loop(0, COHORT, main, 0)
    keep_dq = pltpu.make_async_copy(dqs.at[at128(e), :], dq_ref.at[:, at128(2 * h, PAIR)], out_recv.at[0, e])
    keep_dq.start()

    def tail_part(n, carry):
        earlier = n * ROWS + stream_row < delta + W
        back[at128(n), :] = jnp.where(earlier, acc[1, at128(n), :] * by_half, 0.0).astype(BF16)
        return carry

    lax.fori_loop(0, 16, tail_part, 0)

    def send_tail(n):
        return pltpu.make_async_remote_copy(
            src_ref=tsend.at[at128(n), :], dst_ref=trecv.at[at128(g), :],
            send_sem=tr_send.at[n], recv_sem=tr_recv.at[g],
            device_id={"seq": same_head(n)}, device_id_type=MESH)

    def take_tail(s):
        return pltpu.make_async_remote_copy(
            src_ref=tsend.at[at128(s), :], dst_ref=trecv.at[at128(s), :],
            send_sem=tr_send.at[s], recv_sem=tr_recv.at[s],
            device_id={"seq": same_head(s)}, device_id_type=MESH)

    is_first = (g == 0).astype(F32)

    def unmove(n, carry):
        low = n + whole
        high = low + 1
        low_in = (low >= 0) & (low < 16)
        high_in = (high >= 0) & (high < 16)
        hit = (shift_col == shift_row + part).astype(F32)
        low_hit = (hit[:, :ROWS] * low_in.astype(F32)).astype(BF16)
        high_hit = (hit[:, ROWS:] * high_in.astype(F32)).astype(BF16)
        moved = (dot_nn(low_hit, back[at128(jnp.clip(low, 0, 15)), :])
                 + dot_nn(high_hit, back[at128(jnp.clip(high, 0, 15)), :]))
        tsend[at128(n), :] = (moved + acc[0, at128(n), :] * by_half * is_first).astype(BF16)

        @pl.when(n != g)
        def _():
            send_tail(n).start()

        return carry

    lax.fori_loop(0, COHORT, unmove, 0)

    def send_own(n, kind):
        return pltpu.make_async_remote_copy(
            src_ref=osend.at[at128(n), (left, right)[kind]],
            dst_ref=(dk_ref, dv_ref)[kind].at[:, at128(h)],
            send_sem=out_send.at[1 + kind, n], recv_sem=out_recv.at[1 + kind, e],
            device_id={"seq": g * COHORT + n}, device_id_type=MESH)

    def own(n, carry):
        send_halo_grad(n).wait_recv()
        osend[at128(n), :] = (token_part(COHORT + n) + hrecv[at128(n), :].astype(F32)).astype(BF16)

        @pl.when(n != e)
        def _():
            send_own(n, 0).start()
            send_own(n, 1).start()

        return carry

    lax.fori_loop(0, COHORT, own, 0)

    def keep_own(kind):
        return pltpu.make_async_copy(
            osend.at[at128(e), (left, right)[kind]], (dk_ref, dv_ref)[kind].at[:, at128(h)], out_recv.at[1 + kind, e])

    keep_own(0).start()
    keep_own(1).start()

    def gather_tail(t, carry):
        take_tail((g + t) % COHORT).wait_recv()
        return carry

    lax.fori_loop(1, COHORT, gather_tail, 0)
    trecv[at128(g), :] = tsend[at128(g), :]
    summed = jnp.zeros((ROWS, PAIR), F32)
    for s in range(COHORT):
        summed = summed + trecv[s * ROWS:(s + 1) * ROWS, :].astype(F32)
    tfin[...] = summed.astype(BF16)

    def rows16(n):
        return pl.ds(pl.multiple_of(n * 16, 16), 16)

    def send_tail_out(t, kind):
        to = (e + t) % COHORT
        return pltpu.make_async_remote_copy(
            src_ref=tfin.at[rows16(to), (left, right)[kind]],
            dst_ref=(dtk_ref, dtv_ref)[kind].at[:, at128(h)],
            send_sem=out_send.at[3 + kind, to], recv_sem=out_recv.at[3 + kind, e],
            device_id={"seq": peer(t)}, device_id_type=MESH)

    def keep_tail_out(kind):
        return pltpu.make_async_copy(
            tfin.at[rows16(e), (left, right)[kind]], (dtk_ref, dtv_ref)[kind].at[:, at128(h)], out_recv.at[3 + kind, e])

    def start_tail_out(t, carry):
        send_tail_out(t, 0).start()
        send_tail_out(t, 1).start()
        return carry

    lax.fori_loop(1, COHORT, start_tail_out, 0)
    keep_tail_out(0).start()
    keep_tail_out(1).start()

    def finish(t, carry):
        source = (e + t) % COHORT
        head = (source + flip) % COHORT
        for kind in range(6):
            give(kind, t).wait_send()
        tail_give(t).wait_send()
        send_dq(source).wait_send()
        send_own(source, 0).wait_send()
        send_own(source, 1).wait_send()
        send_tail((g + t) % COHORT).wait_send()
        send_tail_out(t, 0).wait_send()
        send_tail_out(t, 1).wait_send()
        for kind, (src, dst) in enumerate((
            (dqs.at[at128(e), :], dq_ref.at[:, at128(2 * head, PAIR)]),
            (osend.at[at128(e), left], dk_ref.at[:, at128(head)]),
            (osend.at[at128(e), right], dv_ref.at[:, at128(head)]),
            (tfin.at[rows16(e), left], dtk_ref.at[:, at128(head)]),
            (tfin.at[rows16(e), right], dtv_ref.at[:, at128(head)]),
        )):
            pltpu.make_async_remote_copy(
                src_ref=src, dst_ref=dst, send_sem=out_send.at[kind, source], recv_sem=out_recv.at[kind, source],
                device_id={"seq": peer(t)}, device_id_type=MESH).wait_recv()
        return carry

    lax.fori_loop(1, COHORT, finish, 0)

    def finish_halo(i, carry):
        send_halo_grad(i).wait_send()
        return carry

    lax.fori_loop(0, COHORT, finish_halo, 0)
    halo.wait_send()
    keep_dq.wait()
    keep_own(0).wait()
    keep_own(1).wait()
    keep_tail_out(0).wait()
    keep_tail_out(1).wait()


def on_device(queries, keys, values, dout, tail_keys, tail_values, lengths):
    anywhere = pl.BlockSpec(memory_space=pl.ANY)
    dma = pltpu.SemaphoreType.DMA
    scratch = [
        pltpu.VMEM((W, PAIR), BF16),
        pltpu.VMEM((W, PAIR), BF16),
        pltpu.VMEM((2 * STREAM, PAIR), BF16),
        pltpu.VMEM((W, PAIR), BF16),
        pltpu.VMEM((HD, 2 * STREAM), BF16),
        pltpu.VMEM((BAND, PAIR), F32),
        pltpu.VMEM((BAND, PAIR), F32),
        pltpu.VMEM((BAND, PAIR), BF16),
        pltpu.VMEM((BAND, PAIR), BF16),
        pltpu.VMEM((2, STREAM, PAIR), F32),
        pltpu.VMEM((BAND, PAIR), F32),
        pltpu.VMEM((ROWS, PAIR), F32),
        pltpu.VMEM((STREAM, PAIR), BF16),
        pltpu.VMEM((W, PAIR), BF16),
        pltpu.VMEM((W, PAIR), BF16),
        pltpu.VMEM((W, PAIR), BF16),
        pltpu.VMEM((W, PAIR), BF16),
        pltpu.VMEM((W, PAIR), BF16),
        pltpu.VMEM((W, PAIR), BF16),
        pltpu.VMEM((ROWS, PAIR), BF16),
        dma((6, COHORT)), dma((6, COHORT)), dma((2,)), dma((COHORT,)), dma((COHORT,)),
        dma((COHORT,)), dma((COHORT,)), dma((COHORT,)), dma((COHORT,)), dma((5, COHORT)), dma((5, COHORT)),
    ]
    return pl.pallas_call(
        kernel,
        out_shape=(
            jax.ShapeDtypeStruct(queries.shape, BF16),
            jax.ShapeDtypeStruct(keys.shape, BF16),
            jax.ShapeDtypeStruct(values.shape, BF16),
            jax.ShapeDtypeStruct(tail_keys.shape, BF16),
            jax.ShapeDtypeStruct(tail_values.shape, BF16),
        ),
        in_specs=[pl.BlockSpec(memory_space=pltpu.SMEM)] + [anywhere] * 6,
        out_specs=(anywhere,) * 5,
        scratch_shapes=scratch,
        compiler_params=pltpu.CompilerParams(
            collective_id=0, has_side_effects=True, vmem_limit_bytes=48 * 1024 * 1024),
    )(lengths, queries, dout, keys, values, tail_keys, tail_values)


def solution(mesh):
    rows = P(("grp", "seq"), None)
    return jax.shard_map(
        on_device,
        mesh=mesh,
        in_specs=(rows,) * 6 + (P("grp"),),
        out_specs=(rows,) * 5,
        check_vma=False,
    )
```

```python
import math

import jax
import jax.numpy as jnp
from jax import lax
from jax.experimental import pallas as pl
from jax.experimental.pallas import tpu as pltpu
from jax.sharding import PartitionSpec as P


HD = 128
W = 1024
ROWS = 128
PLANE = 16
PLANES = 4
TOKENS = PLANE * ROWS
PAIR = 2 * HD
BLOCK = 256
BLOCKS = TOKENS // BLOCK
SLOTS = BLOCKS + 1
BAND = W + BLOCK
CHUNKS = BAND // ROWS
STREAM = W + TOKENS
UNITS = STREAM // BLOCK
HALO_UNITS = W // BLOCK
GROUP = 512
SCALE = 168.0 ** -0.5
SCALE2 = SCALE * math.log2(math.e)
NEG = -1.0e30
F32 = jnp.float32
BF16 = jnp.bfloat16
MESH = pl.DeviceIdType.MESH


def dot_nt(a, b):
    return lax.dot_general(a, b, (((1,), (1,)), ((), ())), preferred_element_type=F32)


def dot_nn(a, b):
    return jnp.dot(a, b, preferred_element_type=F32)


def at128(index, count=ROWS):
    return pl.ds(index * ROWS, count)


def at256(index, count=BLOCK):
    return pl.ds(index * BLOCK, count)


def at16(index):
    return pl.ds(pl.multiple_of(index * 16, 16), 16)


def kernel(len_ref, q_ref, do_ref, k_ref, v_ref, tk_ref, tv_ref,
           dq_ref, dk_ref, dv_ref, dtk_ref, dtv_ref,
           qb, dob, kv, tkv, kt, sc, dpc, ds, pr, dsx, prx, qq, oo, dqx,
           tok, back, first_part, xsend, xrecv, hsend, hrecv, osend, dqs,
           txs, txr, tsend, trecv, tfin,
           in_send, in_recv, tg_send, tg_recv, ts_send, ts_recv, halo_send, halo_recv, sh_send, sh_recv,
           x_send, x_recv, hg_send, hg_recv, tx_send, tx_recv, tr_send, tr_recv, out_send, out_recv):
    me = lax.axis_index("seq")
    p = me // PLANE
    e = me % PLANE
    head = e // 2
    core = e % 2
    t0 = p * TOKENS
    mine = pl.ds(core * HD, HD)
    other = pl.ds((1 - core) * HD, HD)
    sibling = me + 1 - 2 * core

    def peer(t):
        return p * PLANE + (e + t) % PLANE

    def in_plane(pp):
        return pp * PLANE + e

    def remote(src, dst, send_sem, recv_sem, device):
        return pltpu.make_async_remote_copy(
            src_ref=src, dst_ref=dst, send_sem=send_sem, recv_sem=recv_sem,
            device_id={"seq": device}, device_id_type=MESH)

    barrier = pltpu.get_barrier_semaphore()

    def greet(t, carry):
        pl.semaphore_signal(barrier, inc=1, device_id={"seq": peer(t)}, device_id_type=MESH)
        return carry

    def greet_plane(t, carry):
        pl.semaphore_signal(barrier, inc=1, device_id={"seq": in_plane((p + t) % PLANES)}, device_id_type=MESH)
        return carry

    lax.fori_loop(1, PLANE, greet, 0)
    lax.fori_loop(1, PLANES, greet_plane, 0)
    pl.semaphore_wait(barrier, PLANE + PLANES - 2)

    def origin(kind, to, role):
        if kind == 0:
            return (tk_ref, tv_ref)[role].at[:, at128(to // 2)]
        if kind == 1:
            return (k_ref, v_ref)[role].at[:, at128(to // 2)]
        return (q_ref, do_ref)[kind - 2].at[:, at128(to)]

    def target(kind, source, role):
        columns = pl.ds(role * HD, HD)
        if kind == 0:
            return tkv.at[at16(p * PLANE + source), columns]
        if kind == 1:
            return kv.at[at128(W // ROWS + source), columns]
        return (qb, dob)[kind - 2].at[at128(source), :]

    def give(kind, t, role):
        to = (e + t) % PLANE
        return remote(origin(kind, to, role), target(kind, e, to % 2),
                      in_send.at[kind, t], in_recv.at[kind, e], peer(t))

    def take(kind, source):
        return remote(origin(kind, e, 0), target(kind, source, core),
                      in_send.at[kind, 0], in_recv.at[kind, source], sibling)

    def keep(kind, role):
        return pltpu.make_async_copy(origin(kind, e, role), target(kind, e, core), in_recv.at[kind, e])

    def by_role(kind, to, act):
        if kind >= 2:
            act(0)
        else:
            for role in range(2):
                @pl.when(to % 2 == role)
                def _(role=role):
                    act(role)

    def give_all(kind):
        def body(t, carry):
            by_role(kind, (e + t) % PLANE, lambda role: give(kind, t, role).start())
            return carry
        lax.fori_loop(1, PLANE, body, 0)
        by_role(kind, e, lambda role: keep(kind, role).start())

    def take_some(kind, low, high):
        def body(source, carry):
            @pl.when(source == e)
            def _():
                keep(kind, 0).wait()

            @pl.when(source != e)
            def _():
                take(kind, source).wait_recv()

            return carry
        lax.fori_loop(low, high, body, 0)

    def tail_give(t):
        rows = at256(p)
        return remote(tkv.at[rows, mine], tkv.at[rows, mine], tg_send.at[t], tg_recv.at[p], in_plane((p + t) % PLANES))

    def tail_take(pp):
        rows = at256(pp)
        return remote(tkv.at[rows, mine], tkv.at[rows, mine], tg_send.at[0], tg_recv.at[pp], in_plane(pp))

    def tail_share(pp):
        rows = at256(pp)
        return remote(tkv.at[rows, mine], tkv.at[rows, mine], ts_send.at[pp], ts_recv.at[pp], sibling)

    def tail_shared(pp):
        rows = at256(pp)
        return remote(tkv.at[rows, mine], tkv.at[rows, other], ts_send.at[pp], ts_recv.at[pp], sibling)

    def halo(k):
        return remote(kv.at[pl.ds(TOKENS + k * GROUP, GROUP), mine], kv.at[pl.ds(k * GROUP, GROUP), mine],
                      halo_send.at[k], halo_recv.at[k], in_plane((p + 1) % PLANES))

    def share(k):
        rows = pl.ds(k * GROUP, GROUP)
        return remote(kv.at[rows, mine], kv.at[rows, mine], sh_send.at[k], sh_recv.at[k], sibling)

    def shared(k):
        rows = pl.ds(k * GROUP, GROUP)
        return remote(kv.at[rows, mine], kv.at[rows, other], sh_send.at[k], sh_recv.at[k], sibling)

    give_all(0)
    give_all(1)
    give_all(2)
    give_all(3)

    take_some(0, 0, PLANE)
    for t in range(1, PLANES):
        tail_give(t).start()
    tail_share(p).start()

    for k in (5, 4, 3, 2):
        take_some(1, 4 * (k - 2), 4 * (k - 1))
        if k >= 4:
            halo(k - 4).start()
        share(k).start()

    edge = jnp.zeros((BLOCK, BLOCK), BF16)
    for ref in (dsx, prx):
        for n in range(19):
            if not 7 <= n < 12:
                ref[n * BLOCK:(n + 1) * BLOCK, :] = edge

    def wait_tail(t, carry):
        pp = (p + t) % PLANES
        tail_take(pp).wait_recv()
        tail_share(pp).start()
        return carry

    lax.fori_loop(1, PLANES, wait_tail, 0)

    def wait_shared_tail(pp, carry):
        tail_shared(pp).wait_recv()
        return carry

    lax.fori_loop(0, PLANES, wait_shared_tail, 0)

    first = len_ref[0]
    delta = first - t0
    whole = lax.shift_right_arithmetic(delta, 7)
    part = delta - whole * ROWS
    shift_row = lax.broadcasted_iota(jnp.int32, (ROWS, 2 * ROWS), 0)
    shift_col = lax.broadcasted_iota(jnp.int32, (ROWS, 2 * ROWS), 1)
    forth = (shift_col == shift_row + (ROWS - part)).astype(F32).astype(BF16)
    stream_row = lax.broadcasted_iota(jnp.int32, (ROWS, PAIR), 0)

    def second_stream(n, carry):
        low = jnp.clip(n - whole - 1, 0, W // ROWS - 1)
        high = jnp.clip(n - whole, 0, W // ROWS - 1)
        moved = (dot_nn(forth[:, :ROWS], tkv[at128(low), :])
                 + dot_nn(forth[:, ROWS:], tkv[at128(high), :]))
        plain = kv[at128(n), :]
        mixed = jnp.where(n * ROWS + stream_row < delta + W, moved, plain.astype(F32)).astype(BF16)
        kv[at128(STREAM // ROWS + n), :] = mixed
        kt[:, at128(n)] = plain[:, :HD].T
        kt[:, at128(STREAM // ROWS + n)] = mixed[:, :HD].T
        return carry

    for k in (5, 4, 3, 2):
        shared(k).wait_recv()
        lax.fori_loop(4 * k, 4 * k + 4, second_stream, 0)

    for k in (1, 0):
        halo(k).wait_recv()
        share(k).start()
        shared(k).wait_recv()
        share(k).wait_send()

        @pl.when(p == 0)
        def _(k=k):
            kv[k * GROUP:(k + 1) * GROUP, :] = tkv[k * GROUP:(k + 1) * GROUP, :]

        lax.fori_loop(4 * k, 4 * k + 4, second_stream, 0)

    key_row = lax.broadcasted_iota(jnp.int32, (ROWS, BLOCK), 0)
    query_row = lax.broadcasted_iota(jnp.int32, (ROWS, BLOCK), 1)
    lane_row = lax.broadcasted_iota(jnp.int32, (1, BLOCK), 1)
    cut = jnp.clip(lax.shift_right_arithmetic(delta, 8), 0, BLOCKS - 1)

    def is_second(i):
        return (i * BLOCK >= delta).astype(jnp.int32)

    def band(block, second, c):
        return at128(2 * block + c + second * (STREAM // ROWS))

    take_some(2, 0, PLANE)

    def slot_place(slot):
        if slot == BLOCKS:
            return cut, jnp.int32(1)
        return slot, is_second(slot)

    def logits_of(slot):
        block, second = slot_place(slot)
        queries = qb[at256(block), :]
        rows = at256(slot)
        qq[rows, :HD] = queries * (1 - second).astype(F32).astype(BF16)
        qq[rows, HD:] = queries * second.astype(F32).astype(BF16)
        top = None
        for c in range(CHUNKS):
            logits = dot_nt(kv[band(block, second, c), :HD], queries)
            if c < 2:
                logits = jnp.where(key_row + c * ROWS > query_row, logits, NEG)
            if c >= CHUNKS - 2:
                logits = jnp.where(key_row + (c * ROWS - W) <= query_row, logits, NEG)
            sc[slot, c * ROWS:(c + 1) * ROWS, :] = logits
            most = jnp.max(logits, axis=0, keepdims=True)
            top = most if top is None else jnp.maximum(top, most)
        return top

    def weigh(slot, top):
        total = jnp.zeros((1, BLOCK), F32)
        for c in range(CHUNKS):
            weight = jnp.exp2((sc[slot, c * ROWS:(c + 1) * ROWS, :] - top) * SCALE2)
            sc[slot, c * ROWS:(c + 1) * ROWS, :] = weight
            total = total + jnp.sum(weight, axis=0, keepdims=True)
        return total

    order = [BLOCKS] + list(range(BLOCKS))
    totals = {}
    tops = {order[0]: logits_of(order[0])}
    for at, slot in enumerate(order):
        if at + 1 < SLOTS:
            tops[order[at + 1]] = logits_of(order[at + 1])
        totals[slot] = weigh(slot, tops[slot])

    take_some(3, 0, PLANE)

    cut_row = lane_row + cut * BLOCK
    in_cut = ((cut_row >= delta) & (cut * BLOCK < delta)).astype(F32)
    inner = 7 * BLOCK

    def turn(slot):
        return 0 if slot == BLOCKS else (slot + 1) % 2

    def dprobs_of(slot):
        block, second = slot_place(slot)
        douts = dob[at256(block), :]
        rows = at256(slot)
        oo[rows, :HD] = douts * (1 - second).astype(F32).astype(BF16)
        oo[rows, HD:] = douts * second.astype(F32).astype(BF16)
        mixed = jnp.zeros((1, BLOCK), F32)
        for c in range(CHUNKS):
            rows = slice(c * ROWS, (c + 1) * ROWS)
            dprob = dot_nt(kv[band(block, second, c), HD:], douts)
            dpc[turn(slot), rows, :] = dprob
            mixed = mixed + jnp.sum(sc[slot, rows, :] * dprob, axis=0, keepdims=True)
        return mixed

    def scores(slot, mixed):
        if slot == BLOCKS:
            valid = in_cut
        else:
            valid = jnp.maximum((lane_row + slot * BLOCK < delta).astype(F32), is_second(slot).astype(F32))
        inverse = valid / totals[slot]
        deltas = mixed / totals[slot]
        for c in range(CHUNKS):
            rows = slice(c * ROWS, (c + 1) * ROWS)
            probs = sc[slot, rows, :] * inverse
            dscores = (probs * (dpc[turn(slot), rows, :] - deltas)).astype(BF16)
            if slot == BLOCKS:
                rows = slice(inner + c * ROWS, inner + (c + 1) * ROWS)
                prx[rows, :] = probs.astype(BF16)
                dsx[rows, :] = dscores
            else:
                pr[slot, rows, :] = probs.astype(BF16)
                ds[slot, rows, :] = dscores

    def query_grad(slot):
        block, second = slot_place(slot)
        keys_t = kt[:, pl.ds(2 * block * ROWS + second * STREAM, BAND)]
        if slot == BLOCKS:
            dqx[...] = (dot_nn(keys_t, dsx[inner:inner + BAND, :]) * SCALE).T
            return
        dq = (dot_nn(keys_t, ds[slot]) * SCALE).T
        dqs[at256(slot), :] = (dq + dqx[...] * (cut == slot).astype(F32)).astype(BF16)

    def send_dq(n):
        return remote(dqs.at[at128(n), :], dq_ref.at[:, at128(e)], out_send.at[0, n], out_recv.at[0, e], p * PLANE + n)

    def swap(u):
        return remote(xsend.at[at256(u), other], xrecv.at[at256(u), :], x_send.at[u], x_recv.at[u], sibling)

    def send_halo_grad(u):
        return remote(hsend.at[at256(u), :], hrecv.at[at256(u), :], hg_send.at[u], hg_recv.at[u],
                      in_plane((p + PLANES - 1) % PLANES))

    def send_own(n, role):
        return remote(osend.at[at128(n), :], (dk_ref, dv_ref)[role].at[:, at128(head)],
                      out_send.at[1, n], out_recv.at[1 + role, head], p * PLANE + n)

    def keep_dq():
        return pltpu.make_async_copy(dqs.at[at128(e), :], dq_ref.at[:, at128(e)], out_recv.at[0, e])

    def keep_own(role):
        return pltpu.make_async_copy(
            osend.at[at128(e), :], (dk_ref, dv_ref)[role].at[:, at128(head)], out_recv.at[1 + role, head])

    has_halo = (p > 0).astype(F32)
    is_first = (p == 0).astype(F32)
    unit_row = lax.broadcasted_iota(jnp.int32, (BLOCK, HD), 0)

    def send_some_dq(n, carry):
        @pl.when(n != e)
        def _():
            send_dq(n).start()

        return carry

    def gather(u):
        low, high = max(0, u - 4), min(BLOCKS - 1, u)
        extra = at256(u + 7 - cut)
        later = u * BLOCK + unit_row >= delta + W
        token = []
        for ref, ref_x, right_side, scale in ((ds, dsx, qq, SCALE), (pr, prx, oo, 1.0)):
            parts = [ref[i, (u - i) * BLOCK:(u - i + 1) * BLOCK, :] for i in range(low, high + 1)]
            both = dot_nn(jnp.concatenate(parts, axis=1), right_side[low * BLOCK:(high + 1) * BLOCK, :])
            both = (both + dot_nn(ref_x[extra, :], right_side[BLOCKS * BLOCK:, :])) * scale
            token.append(both[:, :HD] + jnp.where(later, both[:, HD:], 0.0))
        rows = slice(u * BLOCK, (u + 1) * BLOCK)
        token = jnp.concatenate(token, axis=1)
        tok[u % 4] = token
        xsend[rows, :] = token.astype(BF16)
        swap(u).start()
        if u < HALO_UNITS:
            first_part[rows, :] = (token * is_first).astype(BF16)

    def settle(u):
        swap(u).wait_recv()
        total = tok[u % 4, :, mine] + xrecv[u * BLOCK:(u + 1) * BLOCK, :].astype(F32)
        if u < HALO_UNITS:
            hsend[u * BLOCK:(u + 1) * BLOCK, :] = (total * has_halo).astype(BF16)
            send_halo_grad(u).start()
            return
        v = u - HALO_UNITS
        if v >= BLOCKS - HALO_UNITS:
            w = v - (BLOCKS - HALO_UNITS)
            send_halo_grad(w).wait_recv()
            total = total + hrecv[w * BLOCK:(w + 1) * BLOCK, :].astype(F32)
        osend[v * BLOCK:(v + 1) * BLOCK, :] = total.astype(BF16)
        for n in (2 * v, 2 * v + 1):
            for role in range(2):
                @pl.when((n != e) & (core == role))
                def _(n=n, role=role):
                    send_own(n, role).start()

    base = lax.shift_right_arithmetic(delta, 8)
    lag = delta - base * BLOCK
    back_row = lax.broadcasted_iota(jnp.int32, (BLOCK, 2 * BLOCK), 0)
    back_col = lax.broadcasted_iota(jnp.int32, (BLOCK, 2 * BLOCK), 1)

    def tail_unit(k):
        token = []
        early = (base + k) * BLOCK + unit_row < delta + W
        for ref, ref_x, right_side, scale in ((ds, dsx, qq, SCALE), (pr, prx, oo, 1.0)):
            lefts = [ref_x[inner + k * BLOCK:inner + (k + 1) * BLOCK, :]]
            rights = [right_side[BLOCKS * BLOCK:, HD:]]
            for d in range(k + 1):
                slot = base + d
                inside = ((slot >= 0) & (slot < BLOCKS)).astype(F32).astype(BF16)
                slot = jnp.clip(slot, 0, BLOCKS - 1)
                lefts.append(ref[slot, (k - d) * BLOCK:(k - d + 1) * BLOCK, :])
                rights.append(right_side[at256(slot), HD:] * inside)
            token.append(jnp.where(early, dot_nn(jnp.concatenate(lefts, axis=1), jnp.concatenate(rights, axis=0)) * scale, 0.0))
        back[k * BLOCK:(k + 1) * BLOCK, :] = jnp.concatenate(token, axis=1).astype(BF16)

    def swap_tail(pp):
        return remote(txs.at[at256(pp), other], txr.at[at256(pp), :], tx_send.at[pp], tx_recv.at[pp], sibling)

    def send_tail(pp):
        return remote(tsend.at[at256(pp), :], trecv.at[at256(p), :], tr_send.at[pp], tr_recv.at[p], in_plane(pp))

    def take_tail(pp):
        return remote(tsend.at[at256(pp), :], trecv.at[at256(pp), :], tr_send.at[pp], tr_recv.at[pp], in_plane(pp))

    def start_tail_sums():
        for k in range(W // BLOCK + 1):
            tail_unit(k)
        hit = (back_col == back_row + lag).astype(F32).astype(BF16)
        for pp in range(PLANES):
            rows = slice(pp * BLOCK, (pp + 1) * BLOCK)
            moved = dot_nn(hit, back[pp * BLOCK:(pp + 2) * BLOCK, :])
            txs[rows, :] = (moved + first_part[rows, :].astype(F32)).astype(BF16)
        for pp in range(PLANES):
            swap_tail(pp).start()

    def send_tail_sums():
        for pp in range(PLANES):
            swap_tail(pp).wait_recv()
        for pp in range(PLANES):
            rows = slice(pp * BLOCK, (pp + 1) * BLOCK)
            tsend[rows, :] = (txs[rows, mine].astype(F32) + txr[rows, :].astype(F32)).astype(BF16)
        for pp in range(PLANES):
            @pl.when(p != pp)
            def _(pp=pp):
                send_tail(pp).start()

    mixes = {order[0]: dprobs_of(order[0])}
    for at, slot in enumerate(order):
        if at + 1 < SLOTS:
            mixes[order[at + 1]] = dprobs_of(order[at + 1])
        scores(slot, mixes[slot])
        if at > 0:
            query_grad(order[at - 1])
        if slot in (2, 4, 6):
            lax.fori_loop(2 * slot - 4, 2 * slot, send_some_dq, 0)
        if slot == 3:
            for u in range(4):
                gather(u)
        if slot == 5:
            for u in range(4):
                settle(u)
    query_grad(BLOCKS - 1)
    start_tail_sums()
    lax.fori_loop(12, PLANE, send_some_dq, 0)
    gather(4)
    gather(5)
    send_tail_sums()
    for u in range(6, UNITS):
        gather(u)
        settle(u - 2)
    settle(UNITS - 2)
    keep_dq().start()

    settle(UNITS - 1)
    for role in range(2):
        @pl.when(core == role)
        def _(role=role):
            keep_own(role).start()

    summed = tsend[at256(p), :].astype(F32)
    for t in range(1, PLANES):
        pp = (p + t) % PLANES
        take_tail(pp).wait_recv()
        summed = summed + trecv[at256(pp), :].astype(F32)
    tfin[...] = summed.astype(BF16)

    def send_tail_out(t, role):
        to = (e + t) % PLANE
        return remote(tfin.at[at16(to), :], (dtk_ref, dtv_ref)[role].at[:, at128(head)],
                      out_send.at[2, to], out_recv.at[3 + role, head], peer(t))

    def keep_tail_out(role):
        return pltpu.make_async_copy(
            tfin.at[at16(e), :], (dtk_ref, dtv_ref)[role].at[:, at128(head)], out_recv.at[3 + role, head])

    def start_tail_out(t, carry):
        for role in range(2):
            @pl.when(core == role)
            def _(role=role):
                send_tail_out(t, role).start()
        return carry

    lax.fori_loop(1, PLANE, start_tail_out, 0)
    for role in range(2):
        @pl.when(core == role)
        def _(role=role):
            keep_tail_out(role).start()

    def finish_sends(t, carry):
        n = (e + t) % PLANE
        for kind in range(4):
            give(kind, t, 0).wait_send()
        send_dq(n).wait_send()
        send_own(n, 0).wait_send()
        send_tail_out(t, 0).wait_send()
        remote(dqs.at[at128(e), :], dq_ref.at[:, at128(n)], out_send.at[0, n], out_recv.at[0, n], peer(t)).wait_recv()
        return carry

    lax.fori_loop(1, PLANE, finish_sends, 0)

    def finish_units(u, carry):
        swap(u).wait_send()
        return carry

    lax.fori_loop(0, UNITS, finish_units, 0)

    def finish_halo(k, carry):
        halo(k).wait_send()
        return carry

    lax.fori_loop(0, 2, finish_halo, 0)

    def finish_share(k, carry):
        share(k).wait_send()
        return carry

    lax.fori_loop(2, 6, finish_share, 0)

    def finish_planes(pp, carry):
        send_halo_grad(pp).wait_send()
        tail_share(pp).wait_send()
        swap_tail(pp).wait_send()

        @pl.when(p != pp)
        def _():
            send_tail(pp).wait_send()

        return carry

    lax.fori_loop(0, PLANES, finish_planes, 0)
    for t in range(1, PLANES):
        tail_give(t).wait_send()
    keep_dq().wait()

    def finish_heads(n, carry):
        columns = at128(n)
        for role in range(2):
            @pl.when((n == head) & (core == role))
            def _(role=role):
                keep_own(role).wait()
                keep_tail_out(role).wait()

            @pl.when((n != head) | (core != role))
            def _(role=role):
                remote(osend.at[at128(e), :], (dk_ref, dv_ref)[role].at[:, columns],
                       out_send.at[1, 0], out_recv.at[1 + role, n], sibling).wait_recv()
                remote(tfin.at[at16(e), :], (dtk_ref, dtv_ref)[role].at[:, columns],
                       out_send.at[2, 0], out_recv.at[3 + role, n], sibling).wait_recv()

        return carry

    lax.fori_loop(0, PLANE // 2, finish_heads, 0)


def write_out(*refs):
    for source, target in zip(refs[:5], refs[5:]):
        target[...] = source[...]


def on_device(queries, keys, values, dout, tail_keys, tail_values, lengths):
    anywhere = pl.BlockSpec(memory_space=pl.ANY)
    dma = pltpu.SemaphoreType.DMA
    scratch = [
        pltpu.VMEM((TOKENS, HD), BF16),
        pltpu.VMEM((TOKENS, HD), BF16),
        pltpu.VMEM((2 * STREAM, PAIR), BF16),
        pltpu.VMEM((W, PAIR), BF16),
        pltpu.VMEM((HD, 2 * STREAM), BF16),
        pltpu.VMEM((SLOTS, BAND, BLOCK), F32),
        pltpu.VMEM((2, BAND, BLOCK), F32),
        pltpu.VMEM((BLOCKS, BAND, BLOCK), BF16),
        pltpu.VMEM((BLOCKS, BAND, BLOCK), BF16),
        pltpu.VMEM((19 * BLOCK, BLOCK), BF16),
        pltpu.VMEM((19 * BLOCK, BLOCK), BF16),
        pltpu.VMEM((SLOTS * BLOCK, PAIR), BF16),
        pltpu.VMEM((SLOTS * BLOCK, PAIR), BF16),
        pltpu.VMEM((BLOCK, HD), F32),
        pltpu.VMEM((4, BLOCK, PAIR), F32),
        pltpu.VMEM((W + BLOCK, PAIR), BF16),
        pltpu.VMEM((W, PAIR), BF16),
        pltpu.VMEM((STREAM, PAIR), BF16),
        pltpu.VMEM((STREAM, HD), BF16),
        pltpu.VMEM((W, HD), BF16),
        pltpu.VMEM((W, HD), BF16),
        pltpu.VMEM((TOKENS, HD), BF16),
        pltpu.VMEM((TOKENS, HD), BF16),
        pltpu.VMEM((W, PAIR), BF16),
        pltpu.VMEM((W, HD), BF16),
        pltpu.VMEM((W, HD), BF16),
        pltpu.VMEM((W, HD), BF16),
        pltpu.VMEM((BLOCK, HD), BF16),
        dma((4, PLANE)), dma((4, PLANE)),
        dma((PLANES,)), dma((PLANES,)), dma((PLANES,)), dma((PLANES,)),
        dma((2,)), dma((2,)), dma((6,)), dma((6,)),
        dma((UNITS,)), dma((UNITS,)), dma((PLANES,)), dma((PLANES,)),
        dma((PLANES,)), dma((PLANES,)), dma((PLANES,)), dma((PLANES,)),
        dma((3, PLANE)), dma((5, PLANE)),
    ]
    grads = pl.pallas_call(
        kernel,
        out_shape=(
            jax.ShapeDtypeStruct(queries.shape, BF16),
            jax.ShapeDtypeStruct(keys.shape, BF16),
            jax.ShapeDtypeStruct(values.shape, BF16),
            jax.ShapeDtypeStruct(tail_keys.shape, BF16),
            jax.ShapeDtypeStruct(tail_values.shape, BF16),
        ),
        in_specs=[pl.BlockSpec(memory_space=pltpu.SMEM)] + [anywhere] * 6,
        out_specs=(anywhere,) * 5,
        scratch_shapes=scratch,
        compiler_params=pltpu.CompilerParams(
            collective_id=0, has_side_effects=True, vmem_limit_bytes=62 * 1024 * 1024),
    )(lengths, queries, dout, keys, values, tail_keys, tail_values)
    return pl.pallas_call(
        write_out,
        out_shape=tuple(jax.ShapeDtypeStruct(x.shape, x.dtype) for x in grads),
    )(*grads)


def solution(mesh):
    rows = P(("grp", "seq"), None)
    return jax.shard_map(
        on_device,
        mesh=mesh,
        in_specs=(rows,) * 6 + (P("grp"),),
        out_specs=(rows,) * 5,
        check_vma=False,
    )
```

```python
import math

import jax
import jax.numpy as jnp
from jax import lax
from jax.experimental import pallas as pl
from jax.experimental.pallas import tpu as pltpu
from jax.sharding import PartitionSpec as P


HD = 128
W = 1024
ROWS = 128
PLANE = 16
PLANES = 4
TOKENS = PLANE * ROWS
PAIR = 2 * HD
BLOCK = 256
BLOCKS = TOKENS // BLOCK
SLOTS = BLOCKS + 1
BAND = W + BLOCK
CHUNKS = BAND // ROWS
STREAM = W + TOKENS
UNITS = STREAM // BLOCK
HALO_UNITS = W // BLOCK
GROUP = 512
SCALE = 168.0 ** -0.5
SCALE2 = SCALE * math.log2(math.e)
NEG = -1.0e30
F32 = jnp.float32
BF16 = jnp.bfloat16
MESH = pl.DeviceIdType.MESH


def dot_nt(a, b):
    return lax.dot_general(a, b, (((1,), (1,)), ((), ())), preferred_element_type=F32)


def dot_nn(a, b):
    return jnp.dot(a, b, preferred_element_type=F32)


def at128(index, count=ROWS):
    return pl.ds(index * ROWS, count)


def at256(index, count=BLOCK):
    return pl.ds(index * BLOCK, count)


def at16(index):
    return pl.ds(pl.multiple_of(index * 16, 16), 16)


def kernel(len_ref, q_ref, do_ref, k_ref, v_ref, tk_ref, tv_ref,
           dq_ref, dk_ref, dv_ref, dtk_ref, dtv_ref,
           qb, dob, kv, kvh, tkv, kt, sc, dpc, ds, pr, dsx, prx, qq, oo, dqx,
           tok, back, first_part, xsend, xrecv, hsend, hrecv, osend, dqs,
           txs, txr, tsend, trecv, tfin,
           in_send, in_recv, tg_send, tg_recv, ts_send, ts_recv, halo_send, halo_recv, sh_send, sh_recv,
           x_send, x_recv, hg_send, hg_recv, tx_send, tx_recv, tr_send, tr_recv, out_send, out_recv):
    me = lax.axis_index("seq")
    p = me // PLANE
    e = me % PLANE
    head = e // 2
    core = e % 2
    t0 = p * TOKENS
    sibling = me + 1 - 2 * core

    def peer(t):
        return p * PLANE + (e + t) % PLANE

    def in_plane(pp):
        return pp * PLANE + e

    def remote(src, dst, send_sem, recv_sem, device):
        return pltpu.make_async_remote_copy(
            src_ref=src, dst_ref=dst, send_sem=send_sem, recv_sem=recv_sem,
            device_id={"seq": device}, device_id_type=MESH)

    barrier = pltpu.get_barrier_semaphore()

    def greet(t, carry):
        pl.semaphore_signal(barrier, inc=1, device_id={"seq": peer(t)}, device_id_type=MESH)
        return carry

    def greet_plane(t, carry):
        pl.semaphore_signal(barrier, inc=1, device_id={"seq": in_plane((p + t) % PLANES)}, device_id_type=MESH)
        return carry

    lax.fori_loop(1, PLANE, greet, 0)
    lax.fori_loop(1, PLANES, greet_plane, 0)
    pl.semaphore_wait(barrier, PLANE + PLANES - 2)

    def origin(kind, to, role):
        if kind == 0:
            return (tk_ref, tv_ref)[role].at[:, at128(to // 2)]
        if kind == 1:
            return (k_ref, v_ref)[role].at[:, at128(to // 2)]
        return (q_ref, do_ref)[kind - 2].at[:, at128(to)]

    def target(kind, source, role):
        if kind == 0:
            return tkv.at[role, at16(p * PLANE + source), :]
        if kind == 1:
            return kv.at[role, at128(W // ROWS + source), :]
        return (qb, dob)[kind - 2].at[at128(source), :]

    def give(kind, t, role):
        to = (e + t) % PLANE
        return remote(origin(kind, to, role), target(kind, e, to % 2),
                      in_send.at[kind, t], in_recv.at[kind, e], peer(t))

    def take(kind, source):
        return remote(origin(kind, e, 0), target(kind, source, core),
                      in_send.at[kind, 0], in_recv.at[kind, source], sibling)

    def keep(kind, role):
        return pltpu.make_async_copy(origin(kind, e, role), target(kind, e, core), in_recv.at[kind, e])

    def by_role(kind, to, act):
        if kind >= 2:
            act(0)
        else:
            for role in range(2):
                @pl.when(to % 2 == role)
                def _(role=role):
                    act(role)

    def give_all(kind):
        def body(t, carry):
            by_role(kind, (e + t) % PLANE, lambda role: give(kind, t, role).start())
            return carry
        lax.fori_loop(1, PLANE, body, 0)
        by_role(kind, e, lambda role: keep(kind, role).start())

    def take_some(kind, low, high):
        def body(source, carry):
            @pl.when(source == e)
            def _():
                keep(kind, 0).wait()

            @pl.when(source != e)
            def _():
                take(kind, source).wait_recv()

            return carry
        lax.fori_loop(low, high, body, 0)

    def tail_give(t):
        rows = at256(p)
        return remote(tkv.at[core, rows, :], tkv.at[core, rows, :], tg_send.at[t], tg_recv.at[p], in_plane((p + t) % PLANES))

    def tail_take(pp):
        rows = at256(pp)
        return remote(tkv.at[core, rows, :], tkv.at[core, rows, :], tg_send.at[0], tg_recv.at[pp], in_plane(pp))

    def tail_share(pp):
        rows = at256(pp)
        return remote(tkv.at[core, rows, :], tkv.at[core, rows, :], ts_send.at[pp], ts_recv.at[pp], sibling)

    def tail_shared(pp):
        rows = at256(pp)
        return remote(tkv.at[core, rows, :], tkv.at[1 - core, rows, :], ts_send.at[pp], ts_recv.at[pp], sibling)

    def halo(k):
        return remote(kv.at[core, pl.ds(TOKENS + k * GROUP, GROUP), :], kvh.at[core, pl.ds(k * GROUP, GROUP), :],
                      halo_send.at[k], halo_recv.at[k], in_plane((p + 1) % PLANES))

    def shared_ref(k):
        return kvh if isinstance(k, int) and k < 2 else kv

    def share(k):
        rows = pl.ds(k * GROUP, GROUP)
        ref = shared_ref(k)
        return remote(ref.at[core, rows, :], ref.at[core, rows, :], sh_send.at[k], sh_recv.at[k], sibling)

    def shared(k):
        rows = pl.ds(k * GROUP, GROUP)
        ref = shared_ref(k)
        return remote(ref.at[core, rows, :], ref.at[1 - core, rows, :], sh_send.at[k], sh_recv.at[k], sibling)

    give_all(0)
    give_all(1)

    take_some(0, 0, PLANE)
    for t in range(1, PLANES):
        tail_give(t).start()
    tail_share(p).start()

    def sent(kind):
        def body(t, carry):
            give(kind, t, 0).wait_send()
            return carry
        lax.fori_loop(1, PLANE, body, 0)

    sent(1)
    give_all(2)

    for k in (5, 4, 3, 2):
        take_some(1, 4 * (k - 2), 4 * (k - 1))
        if k >= 4:
            halo(k - 4).start()
        share(k).start()

    edge = jnp.zeros((BLOCK, BLOCK), BF16)
    for ref in (dsx, prx):
        for n in range(19):
            if not 7 <= n < 12:
                ref[n * BLOCK:(n + 1) * BLOCK, :] = edge

    def wait_tail(t, carry):
        pp = (p + t) % PLANES
        tail_take(pp).wait_recv()
        tail_share(pp).start()
        return carry

    lax.fori_loop(1, PLANES, wait_tail, 0)

    def wait_shared_tail(pp, carry):
        tail_shared(pp).wait_recv()
        return carry

    lax.fori_loop(0, PLANES, wait_shared_tail, 0)

    first = len_ref[0]
    delta = first - t0
    whole = lax.shift_right_arithmetic(delta, 7)
    part = delta - whole * ROWS
    shift_row = lax.broadcasted_iota(jnp.int32, (ROWS, 2 * ROWS), 0)
    shift_col = lax.broadcasted_iota(jnp.int32, (ROWS, 2 * ROWS), 1)
    forth = (shift_col == shift_row + (ROWS - part)).astype(F32).astype(BF16)
    stream_row = lax.broadcasted_iota(jnp.int32, (ROWS, PAIR), 0)

    def both(ref, n):
        return jnp.concatenate([ref[0, at128(n), :], ref[1, at128(n), :]], axis=1)

    def second_stream(n):
        low = jnp.clip(n - whole - 1, 0, W // ROWS - 1)
        high = jnp.clip(n - whole, 0, W // ROWS - 1)
        moved = (dot_nn(forth[:, :ROWS], both(tkv, low)) + dot_nn(forth[:, ROWS:], both(tkv, high)))
        plain = both(kvh if n < W // ROWS else kv, n)
        if n < W // ROWS:
            kv[0, at128(n), :] = plain[:, :HD]
            kv[1, at128(n), :] = plain[:, HD:]
        mixed = jnp.where(n * ROWS + stream_row < delta + W, moved, plain.astype(F32)).astype(BF16)
        kv[0, at128(STREAM // ROWS + n), :] = mixed[:, :HD]
        kv[1, at128(STREAM // ROWS + n), :] = mixed[:, HD:]
        kt[:, at128(n)] = plain[:, :HD].T
        kt[:, at128(STREAM // ROWS + n)] = mixed[:, :HD].T

    for k in (5, 4, 3, 2):
        shared(k).wait_recv()
        for n in range(4 * k, 4 * k + 4):
            second_stream(n)
        if k == 5:
            sent(2)
            give_all(3)

    key_row = lax.broadcasted_iota(jnp.int32, (ROWS, BLOCK), 0)
    query_row = lax.broadcasted_iota(jnp.int32, (ROWS, BLOCK), 1)
    lane_row = lax.broadcasted_iota(jnp.int32, (1, BLOCK), 1)
    cut = jnp.clip(lax.shift_right_arithmetic(delta, 8), 0, BLOCKS - 1)

    def is_second(i):
        return (i * BLOCK >= delta).astype(jnp.int32)

    def band(block, second, c):
        return at128(2 * block + c + second * (STREAM // ROWS))

    take_some(2, 0, PLANE)

    def slot_place(slot):
        if slot == BLOCKS:
            return cut, jnp.int32(1)
        return slot, is_second(slot)

    def logits_of(slot):
        block, second = slot_place(slot)
        queries = qb[at256(block), :]
        rows = at256(slot)
        qq[rows, :HD] = queries * (1 - second).astype(F32).astype(BF16)
        qq[rows, HD:] = queries * second.astype(F32).astype(BF16)
        top = None
        for c in range(CHUNKS):
            logits = dot_nt(kv[0, band(block, second, c), :], queries)
            if c < 2:
                logits = jnp.where(key_row + c * ROWS > query_row, logits, NEG)
            if c >= CHUNKS - 2:
                logits = jnp.where(key_row + (c * ROWS - W) <= query_row, logits, NEG)
            sc[slot, c * ROWS:(c + 1) * ROWS, :] = logits
            most = jnp.max(logits, axis=0, keepdims=True)
            top = most if top is None else jnp.maximum(top, most)
        return top

    cut_row = lane_row + cut * BLOCK
    in_cut = ((cut_row >= delta) & (cut * BLOCK < delta)).astype(F32)
    inner = 7 * BLOCK

    def weigh(slot, top):
        total = jnp.zeros((1, BLOCK), F32)
        for c in range(CHUNKS):
            weight = jnp.exp2((sc[slot, c * ROWS:(c + 1) * ROWS, :] - top) * SCALE2)
            sc[slot, c * ROWS:(c + 1) * ROWS, :] = weight
            total = total + jnp.sum(weight, axis=0, keepdims=True)
        if slot == BLOCKS:
            valid = in_cut
        else:
            valid = jnp.maximum((lane_row + slot * BLOCK < delta).astype(F32), is_second(slot).astype(F32))
        inverse = valid / total
        for c in range(CHUNKS):
            rows = slice(c * ROWS, (c + 1) * ROWS)
            probs = sc[slot, rows, :] * inverse
            sc[slot, rows, :] = probs
            if slot == BLOCKS:
                prx[inner + c * ROWS:inner + (c + 1) * ROWS, :] = probs.astype(BF16)
            else:
                pr[slot, rows, :] = probs.astype(BF16)

    def weigh_all(slots):
        top = logits_of(slots[0])
        for at, slot in enumerate(slots):
            after = logits_of(slots[at + 1]) if at + 1 < len(slots) else None
            weigh(slot, top)
            top = after

    weigh_all((7, 6, 5, 4))

    for k in (1, 0):
        halo(k).wait_recv()
        share(k).start()
    for k in (1, 0):
        shared(k).wait_recv()
        share(k).wait_send()

        @pl.when(p == 0)
        def _(k=k):
            kvh[:, k * GROUP:(k + 1) * GROUP, :] = tkv[:, k * GROUP:(k + 1) * GROUP, :]

        for n in range(4 * k, 4 * k + 4):
            second_stream(n)

    weigh_all((3, 2, 1, 0, BLOCKS))

    order = [BLOCKS] + list(range(BLOCKS))
    take_some(3, 0, PLANE)

    def turn(slot):
        return 0 if slot == BLOCKS else (slot + 1) % 2

    def dprobs_of(slot):
        block, second = slot_place(slot)
        douts = dob[at256(block), :]
        rows = at256(slot)
        oo[rows, :HD] = douts * (1 - second).astype(F32).astype(BF16)
        oo[rows, HD:] = douts * second.astype(F32).astype(BF16)
        mixed = jnp.zeros((1, BLOCK), F32)
        for c in range(CHUNKS):
            rows = slice(c * ROWS, (c + 1) * ROWS)
            dprob = dot_nt(kv[1, band(block, second, c), :], douts)
            dpc[turn(slot), rows, :] = dprob
            mixed = mixed + jnp.sum(sc[slot, rows, :] * dprob, axis=0, keepdims=True)
        return mixed

    def scores(slot, deltas):
        for c in range(CHUNKS):
            rows = slice(c * ROWS, (c + 1) * ROWS)
            dscores = (sc[slot, rows, :] * (dpc[turn(slot), rows, :] - deltas)).astype(BF16)
            if slot == BLOCKS:
                dsx[inner + c * ROWS:inner + (c + 1) * ROWS, :] = dscores
            else:
                ds[slot, rows, :] = dscores

    def query_grad(slot):
        block, second = slot_place(slot)
        keys_t = kt[:, pl.ds(2 * block * ROWS + second * STREAM, BAND)]
        if slot == BLOCKS:
            dqx[...] = (dot_nn(keys_t, dsx[inner:inner + BAND, :]) * SCALE).T
            return
        dq = (dot_nn(keys_t, ds[slot]) * SCALE).T
        dqs[at256(slot), :] = (dq + dqx[...] * (cut == slot).astype(F32)).astype(BF16)

    def send_dq(n):
        return remote(dqs.at[at128(n), :], dq_ref.at[:, at128(e)], out_send.at[0, n], out_recv.at[0, e], p * PLANE + n)

    def swap(u):
        return remote(xsend.at[1 - core, at256(u), :], xrecv.at[at256(u), :], x_send.at[u], x_recv.at[u], sibling)

    def send_halo_grad(u):
        return remote(hsend.at[at256(u), :], hrecv.at[at256(u), :], hg_send.at[u], hg_recv.at[u],
                      in_plane((p + PLANES - 1) % PLANES))

    def send_own(n, role):
        return remote(osend.at[at128(n), :], (dk_ref, dv_ref)[role].at[:, at128(head)],
                      out_send.at[1, n], out_recv.at[1 + role, head], p * PLANE + n)

    def keep_dq():
        return pltpu.make_async_copy(dqs.at[at128(e), :], dq_ref.at[:, at128(e)], out_recv.at[0, e])

    def keep_own(role):
        return pltpu.make_async_copy(
            osend.at[at128(e), :], (dk_ref, dv_ref)[role].at[:, at128(head)], out_recv.at[1 + role, head])

    has_halo = (p > 0).astype(F32)
    is_first = (p == 0).astype(F32)
    unit_row = lax.broadcasted_iota(jnp.int32, (BLOCK, HD), 0)

    def send_some_dq(n, carry):
        @pl.when(n != e)
        def _():
            send_dq(n).start()

        return carry

    def gather(u):
        low, high = max(0, u - 4), min(BLOCKS - 1, u)
        extra = at256(u + 7 - cut)
        later = u * BLOCK + unit_row >= delta + W
        token = []
        for ref, ref_x, right_side, scale in ((ds, dsx, qq, SCALE), (pr, prx, oo, 1.0)):
            parts = [ref[i, (u - i) * BLOCK:(u - i + 1) * BLOCK, :] for i in range(low, high + 1)]
            sides = dot_nn(jnp.concatenate(parts, axis=1), right_side[low * BLOCK:(high + 1) * BLOCK, :])
            sides = (sides + dot_nn(ref_x[extra, :], right_side[BLOCKS * BLOCK:, :])) * scale
            token.append(sides[:, :HD] + jnp.where(later, sides[:, HD:], 0.0))
        rows = slice(u * BLOCK, (u + 1) * BLOCK)
        for kind in range(2):
            tok[u % 4, kind] = token[kind]
            xsend[kind, rows, :] = token[kind].astype(BF16)
            if u < HALO_UNITS:
                first_part[rows, kind * HD:(kind + 1) * HD] = (token[kind] * is_first).astype(BF16)
        swap(u).start()

    def settle(u):
        swap(u).wait_recv()
        total = tok[u % 4, core] + xrecv[u * BLOCK:(u + 1) * BLOCK, :].astype(F32)
        if u < HALO_UNITS:
            hsend[u * BLOCK:(u + 1) * BLOCK, :] = (total * has_halo).astype(BF16)
            send_halo_grad(u).start()
            return
        v = u - HALO_UNITS
        if v >= BLOCKS - HALO_UNITS:
            w = v - (BLOCKS - HALO_UNITS)
            send_halo_grad(w).wait_recv()
            total = total + hrecv[w * BLOCK:(w + 1) * BLOCK, :].astype(F32)
        osend[v * BLOCK:(v + 1) * BLOCK, :] = total.astype(BF16)
        for n in (2 * v, 2 * v + 1):
            for role in range(2):
                @pl.when((n != e) & (core == role))
                def _(n=n, role=role):
                    send_own(n, role).start()

    base = lax.shift_right_arithmetic(delta, 8)
    lag = delta - base * BLOCK
    back_row = lax.broadcasted_iota(jnp.int32, (BLOCK, 2 * BLOCK), 0)
    back_col = lax.broadcasted_iota(jnp.int32, (BLOCK, 2 * BLOCK), 1)

    def tail_unit(k):
        token = []
        early = (base + k) * BLOCK + unit_row < delta + W
        for ref, ref_x, right_side, scale in ((ds, dsx, qq, SCALE), (pr, prx, oo, 1.0)):
            lefts = [ref_x[inner + k * BLOCK:inner + (k + 1) * BLOCK, :]]
            rights = [right_side[BLOCKS * BLOCK:, HD:]]
            for d in range(k + 1):
                slot = base + d
                inside = ((slot >= 0) & (slot < BLOCKS)).astype(F32).astype(BF16)
                slot = jnp.clip(slot, 0, BLOCKS - 1)
                lefts.append(ref[slot, (k - d) * BLOCK:(k - d + 1) * BLOCK, :])
                rights.append(right_side[at256(slot), HD:] * inside)
            token.append(jnp.where(early, dot_nn(jnp.concatenate(lefts, axis=1), jnp.concatenate(rights, axis=0)) * scale, 0.0))
        back[k * BLOCK:(k + 1) * BLOCK, :] = jnp.concatenate(token, axis=1).astype(BF16)

    def swap_tail(pp):
        return remote(txs.at[1 - core, at256(pp), :], txr.at[at256(pp), :], tx_send.at[pp], tx_recv.at[pp], sibling)

    def send_tail(pp):
        return remote(tsend.at[at256(pp), :], trecv.at[at256(p), :], tr_send.at[pp], tr_recv.at[p], in_plane(pp))

    def take_tail(pp):
        return remote(tsend.at[at256(pp), :], trecv.at[at256(pp), :], tr_send.at[pp], tr_recv.at[pp], in_plane(pp))

    def start_tail_sums():
        for k in range(W // BLOCK + 1):
            tail_unit(k)
        hit = (back_col == back_row + lag).astype(F32).astype(BF16)
        for pp in range(PLANES):
            rows = slice(pp * BLOCK, (pp + 1) * BLOCK)
            moved = dot_nn(hit, back[pp * BLOCK:(pp + 2) * BLOCK, :])
            moved = (moved + first_part[rows, :].astype(F32)).astype(BF16)
            txs[0, rows, :] = moved[:, :HD]
            txs[1, rows, :] = moved[:, HD:]
        for pp in range(PLANES):
            swap_tail(pp).start()

    def send_tail_sums():
        for pp in range(PLANES):
            swap_tail(pp).wait_recv()
        for pp in range(PLANES):
            rows = slice(pp * BLOCK, (pp + 1) * BLOCK)
            tsend[rows, :] = (txs[core, rows, :].astype(F32) + txr[rows, :].astype(F32)).astype(BF16)
        for pp in range(PLANES):
            @pl.when(p != pp)
            def _(pp=pp):
                send_tail(pp).start()

    mixes = {order[0]: dprobs_of(order[0])}
    for at, slot in enumerate(order):
        if at + 1 < SLOTS:
            mixes[order[at + 1]] = dprobs_of(order[at + 1])
        scores(slot, mixes[slot])
        if at > 0:
            query_grad(order[at - 1])
        if slot in (2, 4, 6):
            lax.fori_loop(2 * slot - 4, 2 * slot, send_some_dq, 0)
        if slot == 3:
            for u in range(4):
                gather(u)
        if slot == 5:
            for u in range(4):
                settle(u)
            gather(4)
            gather(5)
    query_grad(BLOCKS - 1)
    start_tail_sums()
    lax.fori_loop(12, PLANE, send_some_dq, 0)
    gather(6)
    gather(7)
    settle(4)
    settle(5)
    send_tail_sums()
    for u in range(8, UNITS):
        gather(u)
        settle(u - 2)
    settle(UNITS - 2)
    keep_dq().start()

    settle(UNITS - 1)
    for role in range(2):
        @pl.when(core == role)
        def _(role=role):
            keep_own(role).start()

    summed = tsend[at256(p), :].astype(F32)
    for t in range(1, PLANES):
        pp = (p + t) % PLANES
        take_tail(pp).wait_recv()
        summed = summed + trecv[at256(pp), :].astype(F32)
    tfin[...] = summed.astype(BF16)

    def send_tail_out(t, role):
        to = (e + t) % PLANE
        return remote(tfin.at[at16(to), :], (dtk_ref, dtv_ref)[role].at[:, at128(head)],
                      out_send.at[2, to], out_recv.at[3 + role, head], peer(t))

    def keep_tail_out(role):
        return pltpu.make_async_copy(
            tfin.at[at16(e), :], (dtk_ref, dtv_ref)[role].at[:, at128(head)], out_recv.at[3 + role, head])

    def start_tail_out(t, carry):
        for role in range(2):
            @pl.when(core == role)
            def _(role=role):
                send_tail_out(t, role).start()
        return carry

    lax.fori_loop(1, PLANE, start_tail_out, 0)
    for role in range(2):
        @pl.when(core == role)
        def _(role=role):
            keep_tail_out(role).start()

    def finish_sends(t, carry):
        n = (e + t) % PLANE
        for kind in (0, 3):
            give(kind, t, 0).wait_send()
        send_dq(n).wait_send()
        send_own(n, 0).wait_send()
        send_tail_out(t, 0).wait_send()
        remote(dqs.at[at128(e), :], dq_ref.at[:, at128(n)], out_send.at[0, n], out_recv.at[0, n], peer(t)).wait_recv()
        return carry

    lax.fori_loop(1, PLANE, finish_sends, 0)

    def finish_units(u, carry):
        swap(u).wait_send()
        return carry

    lax.fori_loop(0, UNITS, finish_units, 0)

    def finish_halo(k, carry):
        halo(k).wait_send()
        return carry

    lax.fori_loop(0, 2, finish_halo, 0)

    def finish_share(k, carry):
        share(k).wait_send()
        return carry

    lax.fori_loop(2, 6, finish_share, 0)

    def finish_planes(pp, carry):
        send_halo_grad(pp).wait_send()
        tail_share(pp).wait_send()
        swap_tail(pp).wait_send()

        @pl.when(p != pp)
        def _():
            send_tail(pp).wait_send()

        return carry

    lax.fori_loop(0, PLANES, finish_planes, 0)
    for t in range(1, PLANES):
        tail_give(t).wait_send()
    keep_dq().wait()

    def finish_heads(n, carry):
        columns = at128(n)
        for role in range(2):
            @pl.when((n == head) & (core == role))
            def _(role=role):
                keep_own(role).wait()
                keep_tail_out(role).wait()

            @pl.when((n != head) | (core != role))
            def _(role=role):
                remote(osend.at[at128(e), :], (dk_ref, dv_ref)[role].at[:, columns],
                       out_send.at[1, 0], out_recv.at[1 + role, n], sibling).wait_recv()
                remote(tfin.at[at16(e), :], (dtk_ref, dtv_ref)[role].at[:, columns],
                       out_send.at[2, 0], out_recv.at[3 + role, n], sibling).wait_recv()

        return carry

    lax.fori_loop(0, PLANE // 2, finish_heads, 0)


def write_out(*refs):
    for source, target in zip(refs[:5], refs[5:]):
        target[...] = source[...]


def on_device(queries, keys, values, dout, tail_keys, tail_values, lengths):
    anywhere = pl.BlockSpec(memory_space=pl.ANY)
    dma = pltpu.SemaphoreType.DMA
    scratch = [
        pltpu.VMEM((TOKENS, HD), BF16),
        pltpu.VMEM((TOKENS, HD), BF16),
        pltpu.VMEM((2, 2 * STREAM, HD), BF16),
        pltpu.VMEM((2, W, HD), BF16),
        pltpu.VMEM((2, W, HD), BF16),
        pltpu.VMEM((HD, 2 * STREAM), BF16),
        pltpu.VMEM((SLOTS, BAND, BLOCK), F32),
        pltpu.VMEM((2, BAND, BLOCK), F32),
        pltpu.VMEM((BLOCKS, BAND, BLOCK), BF16),
        pltpu.VMEM((BLOCKS, BAND, BLOCK), BF16),
        pltpu.VMEM((19 * BLOCK, BLOCK), BF16),
        pltpu.VMEM((19 * BLOCK, BLOCK), BF16),
        pltpu.VMEM((SLOTS * BLOCK, PAIR), BF16),
        pltpu.VMEM((SLOTS * BLOCK, PAIR), BF16),
        pltpu.VMEM((BLOCK, HD), F32),
        pltpu.VMEM((4, 2, BLOCK, HD), F32),
        pltpu.VMEM((W + BLOCK, PAIR), BF16),
        pltpu.VMEM((W, PAIR), BF16),
        pltpu.VMEM((2, STREAM, HD), BF16),
        pltpu.VMEM((STREAM, HD), BF16),
        pltpu.VMEM((W, HD), BF16),
        pltpu.VMEM((W, HD), BF16),
        pltpu.VMEM((TOKENS, HD), BF16),
        pltpu.VMEM((TOKENS, HD), BF16),
        pltpu.VMEM((2, W, HD), BF16),
        pltpu.VMEM((W, HD), BF16),
        pltpu.VMEM((W, HD), BF16),
        pltpu.VMEM((W, HD), BF16),
        pltpu.VMEM((BLOCK, HD), BF16),
        dma((4, PLANE)), dma((4, PLANE)),
        dma((PLANES,)), dma((PLANES,)), dma((PLANES,)), dma((PLANES,)),
        dma((2,)), dma((2,)), dma((6,)), dma((6,)),
        dma((UNITS,)), dma((UNITS,)), dma((PLANES,)), dma((PLANES,)),
        dma((PLANES,)), dma((PLANES,)), dma((PLANES,)), dma((PLANES,)),
        dma((3, PLANE)), dma((5, PLANE)),
    ]
    grads = pl.pallas_call(
        kernel,
        out_shape=(
            jax.ShapeDtypeStruct(queries.shape, BF16),
            jax.ShapeDtypeStruct(keys.shape, BF16),
            jax.ShapeDtypeStruct(values.shape, BF16),
            jax.ShapeDtypeStruct(tail_keys.shape, BF16),
            jax.ShapeDtypeStruct(tail_values.shape, BF16),
        ),
        in_specs=[pl.BlockSpec(memory_space=pltpu.SMEM)] + [anywhere] * 6,
        out_specs=(anywhere,) * 5,
        scratch_shapes=scratch,
        compiler_params=pltpu.CompilerParams(
            collective_id=0, has_side_effects=True, vmem_limit_bytes=62 * 1024 * 1024),
    )(lengths, queries, dout, keys, values, tail_keys, tail_values)
    return pl.pallas_call(
        write_out,
        out_shape=tuple(jax.ShapeDtypeStruct(x.shape, x.dtype) for x in grads),
    )(*grads)


def solution(mesh):
    rows = P(("grp", "seq"), None)
    return jax.shard_map(
        on_device,
        mesh=mesh,
        in_specs=(rows,) * 6 + (P("grp"),),
        out_specs=(rows,) * 5,
        check_vma=False,
    )
```

```python
import math

import jax
import jax.numpy as jnp
from jax import lax
from jax.experimental import pallas as pl
from jax.experimental.pallas import tpu as pltpu
from jax.sharding import PartitionSpec as P


HD = 128
W = 1024
ROWS = 128
PLANE = 16
PLANES = 4
TOKENS = PLANE * ROWS
PAIR = 2 * HD
BLOCK = 256
BLOCKS = TOKENS // BLOCK
SLOTS = BLOCKS + 1
BAND = W + BLOCK
CHUNKS = BAND // ROWS
STREAM = W + TOKENS
UNITS = STREAM // BLOCK
HALO_UNITS = W // BLOCK
GROUP = 512
SCALE = 168.0 ** -0.5
SCALE2 = SCALE * math.log2(math.e)
NEG = -1.0e30
F32 = jnp.float32
BF16 = jnp.bfloat16
MESH = pl.DeviceIdType.MESH


def dot_nt(a, b):
    return lax.dot_general(a, b, (((1,), (1,)), ((), ())), preferred_element_type=F32)


def dot_nn(a, b):
    return jnp.dot(a, b, preferred_element_type=F32)


def at128(index, count=ROWS):
    return pl.ds(index * ROWS, count)


def at256(index, count=BLOCK):
    return pl.ds(index * BLOCK, count)


def at16(index):
    return pl.ds(pl.multiple_of(index * 16, 16), 16)


def kernel(len_ref, q_ref, do_ref, k_ref, v_ref, tk_ref, tv_ref,
           dq_ref, dk_ref, dv_ref, dtk_ref, dtv_ref,
           qb, dob, kv, kvh, tkv, kt, sc, dpc, ds, pr, dsx, prx, qq, oo, dqx,
           tok, back, first_part, xsend, xrecv, hsend, hrecv, osend, dqs,
           txs, txr, tsend, trecv, tfin,
           in_send, in_recv, tg_send, tg_recv, ts_send, ts_recv, halo_send, halo_recv, sh_send, sh_recv,
           x_send, x_recv, hg_send, hg_recv, tx_send, tx_recv, tr_send, tr_recv, out_send, out_recv):
    me = lax.axis_index("seq")
    p = me // PLANE
    e = me % PLANE
    head = e // 2
    core = e % 2
    t0 = p * TOKENS
    sibling = me + 1 - 2 * core

    def peer(t):
        return p * PLANE + (e + t) % PLANE

    def in_plane(pp):
        return pp * PLANE + e

    def remote(src, dst, send_sem, recv_sem, device):
        return pltpu.make_async_remote_copy(
            src_ref=src, dst_ref=dst, send_sem=send_sem, recv_sem=recv_sem,
            device_id={"seq": device}, device_id_type=MESH)

    barrier = pltpu.get_barrier_semaphore()

    def greet(t, carry):
        pl.semaphore_signal(barrier, inc=1, device_id={"seq": peer(t)}, device_id_type=MESH)
        return carry

    def greet_plane(t, carry):
        pl.semaphore_signal(barrier, inc=1, device_id={"seq": in_plane((p + t) % PLANES)}, device_id_type=MESH)
        return carry

    lax.fori_loop(1, PLANE, greet, 0)
    lax.fori_loop(1, PLANES, greet_plane, 0)
    pl.semaphore_wait(barrier, PLANE + PLANES - 2)

    def origin(kind, to, role):
        if kind == 0:
            return (tk_ref, tv_ref)[role].at[:, at128(to // 2)]
        if kind == 1:
            return (k_ref, v_ref)[role].at[:, at128(to // 2)]
        return (q_ref, do_ref)[kind - 2].at[:, at128(to)]

    def target(kind, source, role):
        if kind == 0:
            return tkv.at[role, at16(p * PLANE + source), :]
        if kind == 1:
            return kv.at[role, at128(W // ROWS + source), :]
        return (qb, dob)[kind - 2].at[at128(source), :]

    def give(kind, t, role):
        to = (e + t) % PLANE
        return remote(origin(kind, to, role), target(kind, e, to % 2),
                      in_send.at[kind, t], in_recv.at[kind, e], peer(t))

    def take(kind, source):
        return remote(origin(kind, e, 0), target(kind, source, core),
                      in_send.at[kind, 0], in_recv.at[kind, source], sibling)

    def keep(kind, role):
        return pltpu.make_async_copy(origin(kind, e, role), target(kind, e, core), in_recv.at[kind, e])

    def by_role(kind, to, act):
        if kind >= 2:
            act(0)
        else:
            for role in range(2):
                @pl.when(to % 2 == role)
                def _(role=role):
                    act(role)

    def give_all(kind):
        def body(t, carry):
            by_role(kind, (e + t) % PLANE, lambda role: give(kind, t, role).start())
            return carry
        lax.fori_loop(1, PLANE, body, 0)
        by_role(kind, e, lambda role: keep(kind, role).start())

    def take_some(kind, low, high):
        def body(source, carry):
            @pl.when(source == e)
            def _():
                keep(kind, 0).wait()

            @pl.when(source != e)
            def _():
                take(kind, source).wait_recv()

            return carry
        lax.fori_loop(low, high, body, 0)

    def tail_give(t):
        rows = at256(p)
        return remote(tkv.at[core, rows, :], tkv.at[core, rows, :], tg_send.at[t], tg_recv.at[p], in_plane((p + t) % PLANES))

    def tail_take(pp):
        rows = at256(pp)
        return remote(tkv.at[core, rows, :], tkv.at[core, rows, :], tg_send.at[0], tg_recv.at[pp], in_plane(pp))

    def tail_share(pp):
        rows = at256(pp)
        return remote(tkv.at[core, rows, :], tkv.at[core, rows, :], ts_send.at[pp], ts_recv.at[pp], sibling)

    def tail_shared(pp):
        rows = at256(pp)
        return remote(tkv.at[core, rows, :], tkv.at[1 - core, rows, :], ts_send.at[pp], ts_recv.at[pp], sibling)

    def halo(k):
        return remote(kv.at[core, pl.ds(TOKENS + k * GROUP, GROUP), :], kvh.at[core, pl.ds(k * GROUP, GROUP), :],
                      halo_send.at[k], halo_recv.at[k], in_plane((p + 1) % PLANES))

    def shared_ref(k):
        return kvh if isinstance(k, int) and k < 2 else kv

    def share(k):
        rows = pl.ds(k * GROUP, GROUP)
        ref = shared_ref(k)
        return remote(ref.at[core, rows, :], ref.at[core, rows, :], sh_send.at[k], sh_recv.at[k], sibling)

    def shared(k):
        rows = pl.ds(k * GROUP, GROUP)
        ref = shared_ref(k)
        return remote(ref.at[core, rows, :], ref.at[1 - core, rows, :], sh_send.at[k], sh_recv.at[k], sibling)

    give_all(0)
    give_all(1)

    take_some(0, 0, PLANE)
    for t in range(1, PLANES):
        tail_give(t).start()
    tail_share(p).start()

    def sent(kind):
        def body(t, carry):
            give(kind, t, 0).wait_send()
            return carry
        lax.fori_loop(1, PLANE, body, 0)

    sent(1)
    give_all(2)

    for k in (5, 4, 3, 2):
        take_some(1, 4 * (k - 2), 4 * (k - 1))
        if k >= 4:
            halo(k - 4).start()
        share(k).start()

    edge = jnp.zeros((BLOCK, BLOCK), BF16)
    for ref in (dsx, prx):
        for n in range(19):
            if not 7 <= n < 12:
                ref[n * BLOCK:(n + 1) * BLOCK, :] = edge

    def wait_tail(t, carry):
        pp = (p + t) % PLANES
        tail_take(pp).wait_recv()
        tail_share(pp).start()
        return carry

    lax.fori_loop(1, PLANES, wait_tail, 0)

    def wait_shared_tail(pp, carry):
        tail_shared(pp).wait_recv()
        return carry

    lax.fori_loop(0, PLANES, wait_shared_tail, 0)

    first = len_ref[0]
    delta = first - t0
    whole = lax.shift_right_arithmetic(delta, 7)
    part = delta - whole * ROWS
    shift_row = lax.broadcasted_iota(jnp.int32, (ROWS, 2 * ROWS), 0)
    shift_col = lax.broadcasted_iota(jnp.int32, (ROWS, 2 * ROWS), 1)
    forth = (shift_col == shift_row + (ROWS - part)).astype(F32).astype(BF16)
    stream_row = lax.broadcasted_iota(jnp.int32, (ROWS, PAIR), 0)

    def both(ref, n):
        return jnp.concatenate([ref[0, at128(n), :], ref[1, at128(n), :]], axis=1)

    def second_stream(n):
        low = jnp.clip(n - whole - 1, 0, W // ROWS - 1)
        high = jnp.clip(n - whole, 0, W // ROWS - 1)
        moved = (dot_nn(forth[:, :ROWS], both(tkv, low)) + dot_nn(forth[:, ROWS:], both(tkv, high)))
        plain = both(kvh if n < W // ROWS else kv, n)
        if n < W // ROWS:
            kv[0, at128(n), :] = plain[:, :HD]
            kv[1, at128(n), :] = plain[:, HD:]
        mixed = jnp.where(n * ROWS + stream_row < delta + W, moved, plain.astype(F32)).astype(BF16)
        kv[0, at128(STREAM // ROWS + n), :] = mixed[:, :HD]
        kv[1, at128(STREAM // ROWS + n), :] = mixed[:, HD:]
        kt[:, at128(n)] = plain[:, :HD].T
        kt[:, at128(STREAM // ROWS + n)] = mixed[:, :HD].T

    for k in (5, 4, 3, 2):
        shared(k).wait_recv()
        for n in range(4 * k, 4 * k + 4):
            second_stream(n)
        if k == 5:
            sent(2)
            give_all(3)

    key_row = lax.broadcasted_iota(jnp.int32, (ROWS, BLOCK), 0)
    query_row = lax.broadcasted_iota(jnp.int32, (ROWS, BLOCK), 1)
    lane_row = lax.broadcasted_iota(jnp.int32, (1, BLOCK), 1)
    cut = jnp.clip(lax.shift_right_arithmetic(delta, 8), 0, BLOCKS - 1)

    def is_second(i):
        return (i * BLOCK >= delta).astype(jnp.int32)

    def band(block, second, c):
        return at128(2 * block + c + second * (STREAM // ROWS))

    take_some(2, 0, PLANE)

    def slot_place(slot):
        if slot == BLOCKS:
            return cut, jnp.int32(1)
        return slot, is_second(slot)

    def logits_of(slot):
        block, second = slot_place(slot)
        queries = qb[at256(block), :]
        rows = at256(slot)
        qq[rows, :HD] = queries * (1 - second).astype(F32).astype(BF16)
        qq[rows, HD:] = queries * second.astype(F32).astype(BF16)
        top = None
        for c in range(CHUNKS):
            logits = dot_nt(kv[0, band(block, second, c), :], queries)
            if c < 2:
                logits = jnp.where(key_row + c * ROWS > query_row, logits, NEG)
            if c >= CHUNKS - 2:
                logits = jnp.where(key_row + (c * ROWS - W) <= query_row, logits, NEG)
            sc[slot, c * ROWS:(c + 1) * ROWS, :] = logits
            most = jnp.max(logits, axis=0, keepdims=True)
            top = most if top is None else jnp.maximum(top, most)
        return top

    cut_row = lane_row + cut * BLOCK
    in_cut = ((cut_row >= delta) & (cut * BLOCK < delta)).astype(F32)
    inner = 7 * BLOCK

    def weigh(slot, top):
        total = jnp.zeros((1, BLOCK), F32)
        for c in range(CHUNKS):
            weight = jnp.exp2((sc[slot, c * ROWS:(c + 1) * ROWS, :] - top) * SCALE2)
            sc[slot, c * ROWS:(c + 1) * ROWS, :] = weight
            total = total + jnp.sum(weight, axis=0, keepdims=True)
        if slot == BLOCKS:
            valid = in_cut
        else:
            valid = jnp.maximum((lane_row + slot * BLOCK < delta).astype(F32), is_second(slot).astype(F32))
        inverse = valid / total
        for c in range(CHUNKS):
            rows = slice(c * ROWS, (c + 1) * ROWS)
            probs = sc[slot, rows, :] * inverse
            sc[slot, rows, :] = probs
            if slot == BLOCKS:
                prx[inner + c * ROWS:inner + (c + 1) * ROWS, :] = probs.astype(BF16)
            else:
                pr[slot, rows, :] = probs.astype(BF16)

    def weigh_all(slots):
        top = logits_of(slots[0])
        for at, slot in enumerate(slots):
            after = logits_of(slots[at + 1]) if at + 1 < len(slots) else None
            weigh(slot, top)
            top = after

    weigh_all((7, 6, 5, 4))

    for k in (1, 0):
        halo(k).wait_recv()
        share(k).start()
    for k in (1, 0):
        shared(k).wait_recv()
        share(k).wait_send()

        @pl.when(p == 0)
        def _(k=k):
            kvh[:, k * GROUP:(k + 1) * GROUP, :] = tkv[:, k * GROUP:(k + 1) * GROUP, :]

        for n in range(4 * k, 4 * k + 4):
            second_stream(n)

    weigh_all((3, 2, 1, 0, BLOCKS))

    order = [BLOCKS] + list(range(BLOCKS))
    take_some(3, 0, PLANE)

    def turn(slot):
        return 0 if slot == BLOCKS else (slot + 1) % 2

    def dprobs_of(slot):
        block, second = slot_place(slot)
        douts = dob[at256(block), :]
        rows = at256(slot)
        oo[rows, :HD] = douts * (1 - second).astype(F32).astype(BF16)
        oo[rows, HD:] = douts * second.astype(F32).astype(BF16)
        mixed = jnp.zeros((1, BLOCK), F32)
        for c in range(CHUNKS):
            rows = slice(c * ROWS, (c + 1) * ROWS)
            dprob = dot_nt(kv[1, band(block, second, c), :], douts)
            dpc[turn(slot), rows, :] = dprob
            mixed = mixed + jnp.sum(sc[slot, rows, :] * dprob, axis=0, keepdims=True)
        return mixed

    def scores(slot, deltas):
        for c in range(CHUNKS):
            rows = slice(c * ROWS, (c + 1) * ROWS)
            dscores = (sc[slot, rows, :] * (dpc[turn(slot), rows, :] - deltas)).astype(BF16)
            if slot == BLOCKS:
                dsx[inner + c * ROWS:inner + (c + 1) * ROWS, :] = dscores
            else:
                ds[slot, rows, :] = dscores

    def query_grad(slot):
        block, second = slot_place(slot)
        keys_t = kt[:, pl.ds(2 * block * ROWS + second * STREAM, BAND)]
        if slot == BLOCKS:
            dqx[...] = (dot_nn(keys_t, dsx[inner:inner + BAND, :]) * SCALE).T
            return
        dq = (dot_nn(keys_t, ds[slot]) * SCALE).T
        dqs[at256(slot), :] = (dq + dqx[...] * (cut == slot).astype(F32)).astype(BF16)

    def send_dq(n):
        return remote(dqs.at[at128(n), :], dq_ref.at[:, at128(e)], out_send.at[0, n], out_recv.at[0, e], p * PLANE + n)

    def swap(u):
        return remote(xsend.at[1 - core, at256(u), :], xrecv.at[at256(u), :], x_send.at[u], x_recv.at[u], sibling)

    def send_halo_grad(u):
        return remote(hsend.at[at256(u), :], hrecv.at[at256(u), :], hg_send.at[u], hg_recv.at[u],
                      in_plane((p + PLANES - 1) % PLANES))

    def send_own(n, role):
        return remote(osend.at[at128(n), :], (dk_ref, dv_ref)[role].at[:, at128(head)],
                      out_send.at[1, n], out_recv.at[1 + role, head], p * PLANE + n)

    def keep_dq():
        return pltpu.make_async_copy(dqs.at[at128(e), :], dq_ref.at[:, at128(e)], out_recv.at[0, e])

    def keep_own(role):
        return pltpu.make_async_copy(
            osend.at[at128(e), :], (dk_ref, dv_ref)[role].at[:, at128(head)], out_recv.at[1 + role, head])

    has_halo = (p > 0).astype(F32)
    is_first = (p == 0).astype(F32)
    unit_row = lax.broadcasted_iota(jnp.int32, (BLOCK, HD), 0)

    def send_some_dq(n, carry):
        @pl.when(n != e)
        def _():
            send_dq(n).start()

        return carry

    def gather(u):
        low, high = max(0, u - 4), min(BLOCKS - 1, u)
        extra = at256(u + 7 - cut)
        later = u * BLOCK + unit_row >= delta + W
        token = []
        for ref, ref_x, right_side, scale in ((ds, dsx, qq, SCALE), (pr, prx, oo, 1.0)):
            parts = [ref[i, (u - i) * BLOCK:(u - i + 1) * BLOCK, :] for i in range(low, high + 1)]
            sides = dot_nn(jnp.concatenate(parts, axis=1), right_side[low * BLOCK:(high + 1) * BLOCK, :])
            sides = (sides + dot_nn(ref_x[extra, :], right_side[BLOCKS * BLOCK:, :])) * scale
            token.append(sides[:, :HD] + jnp.where(later, sides[:, HD:], 0.0))
        rows = slice(u * BLOCK, (u + 1) * BLOCK)
        for kind in range(2):
            tok[u % 4, kind] = token[kind]
            xsend[kind, rows, :] = token[kind].astype(BF16)
            if u < HALO_UNITS:
                first_part[rows, kind * HD:(kind + 1) * HD] = (token[kind] * is_first).astype(BF16)
        swap(u).start()

    def settle(u):
        swap(u).wait_recv()
        total = tok[u % 4, core] + xrecv[u * BLOCK:(u + 1) * BLOCK, :].astype(F32)
        if u < HALO_UNITS:
            hsend[u * BLOCK:(u + 1) * BLOCK, :] = (total * has_halo).astype(BF16)
            send_halo_grad(u).start()
            return
        v = u - HALO_UNITS
        if v >= BLOCKS - HALO_UNITS:
            w = v - (BLOCKS - HALO_UNITS)
            send_halo_grad(w).wait_recv()
            total = total + hrecv[w * BLOCK:(w + 1) * BLOCK, :].astype(F32)
        osend[v * BLOCK:(v + 1) * BLOCK, :] = total.astype(BF16)
        for n in (2 * v, 2 * v + 1):
            for role in range(2):
                @pl.when((n != e) & (core == role))
                def _(n=n, role=role):
                    send_own(n, role).start()

    base = lax.shift_right_arithmetic(delta, 8)
    lag = delta - base * BLOCK
    back_row = lax.broadcasted_iota(jnp.int32, (BLOCK, 2 * BLOCK), 0)
    back_col = lax.broadcasted_iota(jnp.int32, (BLOCK, 2 * BLOCK), 1)

    def tail_unit(k):
        token = []
        early = (base + k) * BLOCK + unit_row < delta + W
        for ref, ref_x, right_side, scale in ((ds, dsx, qq, SCALE), (pr, prx, oo, 1.0)):
            lefts = [ref_x[inner + k * BLOCK:inner + (k + 1) * BLOCK, :]]
            rights = [right_side[BLOCKS * BLOCK:, HD:]]
            for d in range(k + 1):
                slot = base + d
                inside = ((slot >= 0) & (slot < BLOCKS)).astype(F32).astype(BF16)
                slot = jnp.clip(slot, 0, BLOCKS - 1)
                lefts.append(ref[slot, (k - d) * BLOCK:(k - d + 1) * BLOCK, :])
                rights.append(right_side[at256(slot), HD:] * inside)
            token.append(jnp.where(early, dot_nn(jnp.concatenate(lefts, axis=1), jnp.concatenate(rights, axis=0)) * scale, 0.0))
        back[k * BLOCK:(k + 1) * BLOCK, :] = jnp.concatenate(token, axis=1).astype(BF16)

    def swap_tail(pp):
        return remote(txs.at[1 - core, at256(pp), :], txr.at[at256(pp), :], tx_send.at[pp], tx_recv.at[pp], sibling)

    def send_tail(pp):
        return remote(tsend.at[at256(pp), :], trecv.at[at256(p), :], tr_send.at[pp], tr_recv.at[p], in_plane(pp))

    def take_tail(pp):
        return remote(tsend.at[at256(pp), :], trecv.at[at256(pp), :], tr_send.at[pp], tr_recv.at[pp], in_plane(pp))

    def start_tail_sums():
        for k in range(W // BLOCK + 1):
            tail_unit(k)
        hit = (back_col == back_row + lag).astype(F32).astype(BF16)
        for pp in range(PLANES):
            rows = slice(pp * BLOCK, (pp + 1) * BLOCK)
            moved = dot_nn(hit, back[pp * BLOCK:(pp + 2) * BLOCK, :])
            moved = (moved + first_part[rows, :].astype(F32)).astype(BF16)
            txs[0, rows, :] = moved[:, :HD]
            txs[1, rows, :] = moved[:, HD:]
        for pp in range(PLANES):
            swap_tail(pp).start()

    def send_tail_sums():
        for pp in range(PLANES):
            swap_tail(pp).wait_recv()
        for pp in range(PLANES):
            rows = slice(pp * BLOCK, (pp + 1) * BLOCK)
            tsend[rows, :] = (txs[core, rows, :].astype(F32) + txr[rows, :].astype(F32)).astype(BF16)
        for pp in range(PLANES):
            @pl.when(p != pp)
            def _(pp=pp):
                send_tail(pp).start()

    mixes = {order[0]: dprobs_of(order[0])}
    for at, slot in enumerate(order):
        if at + 1 < SLOTS:
            mixes[order[at + 1]] = dprobs_of(order[at + 1])
        scores(slot, mixes[slot])
        if at > 0:
            query_grad(order[at - 1])
        if slot in (2, 4, 6):
            lax.fori_loop(2 * slot - 4, 2 * slot, send_some_dq, 0)
        if slot == 3:
            for u in range(4):
                gather(u)
        if slot == 5:
            for u in range(4):
                settle(u)
            gather(4)
            gather(5)
    query_grad(BLOCKS - 1)
    start_tail_sums()
    lax.fori_loop(12, PLANE, send_some_dq, 0)
    gather(6)
    gather(7)
    settle(4)
    settle(5)
    send_tail_sums()
    for u in range(8, UNITS):
        gather(u)
        settle(u - 2)
    settle(UNITS - 2)
    keep_dq().start()

    settle(UNITS - 1)
    for role in range(2):
        @pl.when(core == role)
        def _(role=role):
            keep_own(role).start()

    def finish_early(t, carry):
        n = (e + t) % PLANE
        for kind in (0, 3):
            give(kind, t, 0).wait_send()
        send_dq(n).wait_send()
        remote(dqs.at[at128(e), :], dq_ref.at[:, at128(n)], out_send.at[0, n], out_recv.at[0, n], peer(t)).wait_recv()
        return carry

    lax.fori_loop(1, PLANE, finish_early, 0)

    def finish_units(u, carry):
        swap(u).wait_send()
        return carry

    lax.fori_loop(0, UNITS, finish_units, 0)

    def finish_halo(k, carry):
        halo(k).wait_send()
        return carry

    lax.fori_loop(0, 2, finish_halo, 0)

    def finish_share(k, carry):
        share(k).wait_send()
        return carry

    lax.fori_loop(2, 6, finish_share, 0)

    def finish_planes(pp, carry):
        send_halo_grad(pp).wait_send()
        tail_share(pp).wait_send()
        swap_tail(pp).wait_send()
        return carry

    lax.fori_loop(0, PLANES, finish_planes, 0)
    for t in range(1, PLANES):
        tail_give(t).wait_send()
    keep_dq().wait()

    summed = tsend[at256(p), :].astype(F32)
    for t in range(1, PLANES):
        pp = (p + t) % PLANES
        take_tail(pp).wait_recv()
        summed = summed + trecv[at256(pp), :].astype(F32)
    tfin[...] = summed.astype(BF16)

    def send_tail_out(t, role):
        to = (e + t) % PLANE
        return remote(tfin.at[at16(to), :], (dtk_ref, dtv_ref)[role].at[:, at128(head)],
                      out_send.at[2, to], out_recv.at[3 + role, head], peer(t))

    def keep_tail_out(role):
        return pltpu.make_async_copy(
            tfin.at[at16(e), :], (dtk_ref, dtv_ref)[role].at[:, at128(head)], out_recv.at[3 + role, head])

    def start_tail_out(t, carry):
        for role in range(2):
            @pl.when(core == role)
            def _(role=role):
                send_tail_out(t, role).start()
        return carry

    lax.fori_loop(1, PLANE, start_tail_out, 0)
    for role in range(2):
        @pl.when(core == role)
        def _(role=role):
            keep_tail_out(role).start()

    def finish_sends(t, carry):
        send_own((e + t) % PLANE, 0).wait_send()
        send_tail_out(t, 0).wait_send()
        return carry

    lax.fori_loop(1, PLANE, finish_sends, 0)

    def finish_tail(pp, carry):
        @pl.when(p != pp)
        def _():
            send_tail(pp).wait_send()

        return carry

    lax.fori_loop(0, PLANES, finish_tail, 0)

    def finish_heads(n, carry):
        columns = at128(n)
        for role in range(2):
            @pl.when((n == head) & (core == role))
            def _(role=role):
                keep_own(role).wait()
                keep_tail_out(role).wait()

            @pl.when((n != head) | (core != role))
            def _(role=role):
                remote(osend.at[at128(e), :], (dk_ref, dv_ref)[role].at[:, columns],
                       out_send.at[1, 0], out_recv.at[1 + role, n], sibling).wait_recv()
                remote(tfin.at[at16(e), :], (dtk_ref, dtv_ref)[role].at[:, columns],
                       out_send.at[2, 0], out_recv.at[3 + role, n], sibling).wait_recv()

        return carry

    lax.fori_loop(0, PLANE // 2, finish_heads, 0)


def write_out(*refs):
    for source, target in zip(refs[:5], refs[5:]):
        target[...] = source[...]


def on_device(queries, keys, values, dout, tail_keys, tail_values, lengths):
    anywhere = pl.BlockSpec(memory_space=pl.ANY)
    dma = pltpu.SemaphoreType.DMA
    scratch = [
        pltpu.VMEM((TOKENS, HD), BF16),
        pltpu.VMEM((TOKENS, HD), BF16),
        pltpu.VMEM((2, 2 * STREAM, HD), BF16),
        pltpu.VMEM((2, W, HD), BF16),
        pltpu.VMEM((2, W, HD), BF16),
        pltpu.VMEM((HD, 2 * STREAM), BF16),
        pltpu.VMEM((SLOTS, BAND, BLOCK), F32),
        pltpu.VMEM((2, BAND, BLOCK), F32),
        pltpu.VMEM((BLOCKS, BAND, BLOCK), BF16),
        pltpu.VMEM((BLOCKS, BAND, BLOCK), BF16),
        pltpu.VMEM((19 * BLOCK, BLOCK), BF16),
        pltpu.VMEM((19 * BLOCK, BLOCK), BF16),
        pltpu.VMEM((SLOTS * BLOCK, PAIR), BF16),
        pltpu.VMEM((SLOTS * BLOCK, PAIR), BF16),
        pltpu.VMEM((BLOCK, HD), F32),
        pltpu.VMEM((4, 2, BLOCK, HD), F32),
        pltpu.VMEM((W + BLOCK, PAIR), BF16),
        pltpu.VMEM((W, PAIR), BF16),
        pltpu.VMEM((2, STREAM, HD), BF16),
        pltpu.VMEM((STREAM, HD), BF16),
        pltpu.VMEM((W, HD), BF16),
        pltpu.VMEM((W, HD), BF16),
        pltpu.VMEM((TOKENS, HD), BF16),
        pltpu.VMEM((TOKENS, HD), BF16),
        pltpu.VMEM((2, W, HD), BF16),
        pltpu.VMEM((W, HD), BF16),
        pltpu.VMEM((W, HD), BF16),
        pltpu.VMEM((W, HD), BF16),
        pltpu.VMEM((BLOCK, HD), BF16),
        dma((4, PLANE)), dma((4, PLANE)),
        dma((PLANES,)), dma((PLANES,)), dma((PLANES,)), dma((PLANES,)),
        dma((2,)), dma((2,)), dma((6,)), dma((6,)),
        dma((UNITS,)), dma((UNITS,)), dma((PLANES,)), dma((PLANES,)),
        dma((PLANES,)), dma((PLANES,)), dma((PLANES,)), dma((PLANES,)),
        dma((3, PLANE)), dma((5, PLANE)),
    ]
    grads = pl.pallas_call(
        kernel,
        out_shape=(
            jax.ShapeDtypeStruct(queries.shape, BF16),
            jax.ShapeDtypeStruct(keys.shape, BF16),
            jax.ShapeDtypeStruct(values.shape, BF16),
            jax.ShapeDtypeStruct(tail_keys.shape, BF16),
            jax.ShapeDtypeStruct(tail_values.shape, BF16),
        ),
        in_specs=[pl.BlockSpec(memory_space=pltpu.SMEM)] + [anywhere] * 6,
        out_specs=(anywhere,) * 5,
        scratch_shapes=scratch,
        compiler_params=pltpu.CompilerParams(
            collective_id=0, has_side_effects=True, vmem_limit_bytes=62 * 1024 * 1024),
    )(lengths, queries, dout, keys, values, tail_keys, tail_values)
    return pl.pallas_call(
        write_out,
        out_shape=tuple(jax.ShapeDtypeStruct(x.shape, x.dtype) for x in grads),
    )(*grads)


def solution(mesh):
    rows = P(("grp", "seq"), None)
    return jax.shard_map(
        on_device,
        mesh=mesh,
        in_specs=(rows,) * 6 + (P("grp"),),
        out_specs=(rows,) * 5,
        check_vma=False,
    )
```
